256 devices in a mesh: row: 16 (over z, x_hi), col: 16 (over x_lo, y, core).
Axes of the slice: x: 4 (x_hi: 2, x_lo: 2; x = x_hi * 2 + x_lo), y: 4, z: 8, core: 2. Of those that a mesh axis runs over, the one named last changes fastest.
Arguments:
- amplitudes: bfloat16 [4096, 14336], P(('col', 'row')), may hold values from -6 to 6
- integrals: bfloat16 [14336, 14336], P('col', 'row'), may hold values from -0.046875 to 0.046875
Outputs:
- ladder: bfloat16 [4096, 14336], P(('col', 'row'))
The draws below stay inside these ranges and needn't reach their ends.
All inputs are finite; a program needn't handle non-finite values.
Results may differ from the reference program's by a relative error of at most 0.001.
Values may be sent and summed in bfloat16 or wider, within the bound.
A program may use at most 128 MiB of HBM per device.

```python
import jax
import jax.numpy as jnp

IJ = 4096
AB = 14336
CD = 14336


def block_levels(rng, shape, shards, low, high):
    def one(dim, parts):
        heights = jax.random.uniform(jax.random.fold_in(jax.random.fold_in(rng, 6), dim), (parts,), jnp.float32, low / len(shards), high / len(shards))
        return jnp.repeat(jnp.exp(heights), shape[dim] // parts).reshape((-1,) + (1,) * (len(shape) - dim - 1))

    loudness = one(*shards[0])
    for cut in shards[1:]:
        loudness = loudness * one(*cut)
    return loudness


def scatter_about(stream_key, extent, scale, reach, shards=(), kind=jnp.bfloat16):
    array = jax.random.normal(stream_key, extent, jnp.float32) * scale
    if len(shards) > 0:
        array = block_levels(stream_key, extent, shards, -0.22, 0.18) * array
    return jnp.clip(array, min=-reach, max=reach).astype(kind)


def setup_inputs(seed: int = 0) -> dict:
    streams_of = jax.random.split(jax.random.key(seed), 3)
    amplitudes = scatter_about(streams_of[0], (IJ, CD), 1.0, 6.0, ((0, 256),))
    integrals = scatter_about(streams_of[1], (CD, AB), CD ** -0.5, 0.046875, ((0, 16), (1, 16)))
    return {"amplitudes": amplitudes, "integrals": integrals}


def reference(amplitudes, integrals):
    product = jnp.dot(amplitudes, integrals, preferred_element_type=jnp.float32)
    return product.astype(jnp.bfloat16)
```

```python
import functools

import jax
import jax.numpy as jnp
from jax import lax
from jax.experimental import pallas as pl
from jax.experimental.pallas import tpu as pltpu
from jax.sharding import PartitionSpec as P

MESH = pl.DeviceIdType.MESH
BF16, F32 = jnp.bfloat16, jnp.float32

NX, NY, NZ = 4, 4, 8
ROWS = 16
BLOCK = 896
HALF = BLOCK // 2
LANES = 128
CHUNKS = BLOCK // LANES
WIDE = 2 * LANES
PAIR = 2 * BLOCK
DEEP = 4 * BLOCK
SLOTS = (0, 1, -1, 2, -2, 3, -3, 4)
SLOT_OF = {d: s for s, d in enumerate(SLOTS)}
SLOT_ROWS = NY * ROWS
SEMS = 86
AHEAD = 2

PASSES = {
    "a": (0, 2, 0, 3),
    "b": (2, 3, 0, 3),
    "c": (0, 3, 3, 5),
    "d": (3, 4, 0, 5),
    "e": (0, 4, 5, 7),
    "f": (4, 5, 0, 7),
    "g": (0, 5, 7, 8),
    "h": (5, 6, 0, 8),
    "i": (6, 7, 0, 8),
}

ORDER = (
    "B00", "S0", "B01", "S1", "B02", "B10", "A10", "B11", "B12", "A11", "Pa", "B20", "B21", "A20",
    "Qa", "B22", "Pb", "B30", "A21", "Pc", "Ra", "B31", "Qb", "B32", "Pd", "A30", "Qc", "B40", "Rb",
    "B41", "Qd", "A31", "Pe", "Rc", "B42", "Pf", "B50", "Qe", "A40", "Rd", "Pg", "B51", "Qf", "B52",
    "Ph", "Qg", "Re", "B60", "Rf", "B61", "Qh", "Rg", "B62", "Pi", "Rh", "Qi", "Ri",
)


def kernel(a_ref, b_ref, o_ref, amps, ints, part, first, second, final, landed, sems):
    row, col = lax.axis_index("row"), lax.axis_index("col")
    z, x = row // 2, (row % 2) * 2 + col // 8
    y, core = (col // 2) % NY, col % 2

    def at(dx=0, dy=0, dz=0, dk=0):
        xx, yy, zz, kk = (x + dx) % NX, (y + dy) % NY, (z + dz) % NZ, (core + dk) % 2
        return (zz * 2 + xx // 2, (xx % 2) * 8 + yy * 2 + kk)

    names = {}

    def sem(name):
        return names.setdefault(name, len(names))

    def put(send, recv, src, dst, to):
        pltpu.make_async_remote_copy(
            src_ref=src, dst_ref=dst, send_sem=sems.at[sem(("send", send))], recv_sem=sems.at[sem(recv)],
            device_id=to, device_id_type=MESH,
        ).start()

    def wait(name, like):
        pltpu.make_async_copy(like, like, sems.at[sem(name)]).wait()

    def place(j, dx, dk, r0, n):
        xx, kk = (x + dx) % NX, (core + dk) % 2
        rows = pl.multiple_of(((xx % 2) * 2 + kk) * BLOCK + r0, 16)
        return ints.at[j, pl.ds(rows, n), pl.ds(pl.multiple_of((xx // 2) * LANES, LANES), LANES)]

    for h in range(2):
        pltpu.make_async_copy(
            a_ref.at[:, pl.ds(pl.multiple_of(h * 4 * PAIR + y * PAIR, LANES), PAIR)],
            amps.at[pl.ds(pl.multiple_of(y * ROWS, ROWS), ROWS), pl.ds(h * PAIR, PAIR)],
            sems.at[sem("own a")],
        ).start()
    for j in range(CHUNKS):
        pltpu.make_async_copy(b_ref.at[:, pl.ds(j * LANES, LANES)], place(j, 0, 0, 0, BLOCK), sems.at[sem("own b")]).start()

    partners = [at(dx=1), at(dx=-1), at(dk=1)]
    partners += [at(dy=d) for d in range(1, NY)] + [at(dz=d) for d in range(1, NZ)]
    barrier = pltpu.get_barrier_semaphore()
    for to in partners:
        pl.semaphore_signal(barrier, inc=1, device_id=to, device_id_type=MESH)
    pl.semaphore_wait(barrier, len(partners))

    for h in range(2):
        for d in (2, 1, 3):
            yy = (y + d) % NY
            put(
                "spread",
                ("spread", h),
                a_ref.at[:, pl.ds(pl.multiple_of(h * 4 * PAIR + yy * PAIR, LANES), PAIR)],
                amps.at[pl.ds(pl.multiple_of(y * ROWS, ROWS), ROWS), pl.ds(h * PAIR, PAIR)],
                at(dy=d),
            )

    def direct(j):
        for step, (right, left) in enumerate(((0, HALF), (HALF, 0))):
            for dx, r0 in ((1, right), (-1, left)):
                put(
                    ("b", j), ("direct", j, step),
                    b_ref.at[pl.ds(r0, HALF), pl.ds(j * LANES, LANES)], place(j, 0, 0, r0, HALF), at(dx=dx),
                )
        put(("b", j), ("twin", j), b_ref.at[:, pl.ds(j * LANES, LANES)], place(j, 0, 0, 0, BLOCK), at(dk=1))

    for j in range(AHEAD):
        direct(j)

    def shard(d, h):
        return amps.at[pl.ds(SLOT_OF[d] * SLOT_ROWS, SLOT_ROWS), pl.ds(h * PAIR, PAIR)]

    def hand_on(d, h):
        if d < 3 or h == 0:
            put("ring", ("ring", d + 1, h % 2 if d < 3 else 0), shard(d, h), shard(d + 1, h), at(dz=-1))
        if d < 3 or h == 1:
            put("ring", ("ring", d + 1, h % 2 if d < 3 else 0), shard(-d, h), shard(4 if d == 3 else -(d + 1), h), at(dz=1))

    def event_s(h):
        if h == 0:
            wait("own a", amps.at[pl.ds(0, ROWS), :])
            wait("own b", b_ref)
        wait(("spread", h), amps.at[pl.ds(0, 3 * ROWS), pl.ds(0, PAIR)])
        hand_on(0, h)

    def event_a(d, h):
        wait(("ring", d, h), amps.at[pl.ds(0, SLOT_ROWS), :])
        if d < 4:
            hand_on(d, h)

    def event_b(j, step):
        two = ints.at[j, pl.ds(0, BLOCK), pl.ds(0, LANES)]
        if step == 0:
            wait(("direct", j, 0), two)
            for dx, r0 in ((1, 0), (-1, HALF)):
                put(("b", j), ("onward", j), place(j, -dx, 0, r0, HALF), place(j, -dx, 0, r0, HALF), at(dx=dx))
        elif step == 1:
            if j + AHEAD < CHUNKS:
                direct(j + AHEAD)
            wait(("direct", j, 1), two)
            for dx in (-1, 1):
                put(("b", j), ("twin", j), place(j, dx, 0, 0, BLOCK), place(j, dx, 0, 0, BLOCK), at(dk=1))
        else:
            wait(("onward", j), two)
            put(("b", j), ("twin", j), place(j, 2, 0, 0, BLOCK), place(j, 2, 0, 0, BLOCK), at(dk=1))
            wait(("twin", j), ints.at[j, :, pl.ds(0, LANES)])

    up, down, over = (y + 1) % NY, (y - 1) % NY, (y + 2) % NY
    LOW, HIGH = pl.ds(0, LANES), pl.ds(LANES, LANES)

    def event_p(p):
        j0, j1, s0, s1 = PASSES[p]
        js, ss = pl.ds(j0, j1 - j0), pl.ds(s0, s1 - s0)
        lhs = amps.at[pl.ds(s0 * SLOT_ROWS, (s1 - s0) * SLOT_ROWS), :]

        def one(j, carry):
            product = jnp.dot(lhs[...], ints[j], preferred_element_type=F32)
            part[j, ss] = product.reshape(s1 - s0, NY, ROWS, WIDE)
            return carry

        if j1 - j0 == 1:
            one(j0, 0)
        else:
            lax.fori_loop(j0, j1, one, 0)
        put(("p", p), ("far", p), part.at[js, ss, over, :, LOW], first.at[js, 0, ss], at(dy=1))
        put(("p", p), ("far", p), part.at[js, ss, over, :, HIGH], first.at[js, 1, ss], at(dy=-1))
        put(("p", p), ("near", p), part.at[js, ss, up, :, HIGH], second.at[js, 0, ss, :, HIGH], at(dy=1))
        put(("p", p), ("near", p), part.at[js, ss, down, :, LOW], second.at[js, 1, ss, :, LOW], at(dy=-1))

    def event_q(p):
        j0, j1, s0, s1 = PASSES[p]
        js, ss = pl.ds(j0, j1 - j0), pl.ds(s0, s1 - s0)
        wait(("far", p), first.at[js, :, ss])
        first[js, 0, ss] += part[js, ss, up, :, LOW]
        put(("q", p), ("near", p), first.at[js, 0, ss], second.at[js, 0, ss, :, LOW], at(dy=1))
        first[js, 1, ss] += part[js, ss, down, :, HIGH]
        put(("q", p), ("near", p), first.at[js, 1, ss], second.at[js, 1, ss, :, HIGH], at(dy=-1))

    def event_r(p):
        j0, j1, s0, s1 = PASSES[p]
        js, ss = pl.ds(j0, j1 - j0), pl.ds(s0, s1 - s0)
        wait(("near", p), second.at[js, :, ss])
        total = part[js, ss, y] + second[js, 0, ss] + second[js, 1, ss]
        final[js, ss] = total.astype(BF16)
        for s in sorted(range(s0, s1), key=lambda s: -abs(SLOTS[s])):
            if s == 0:
                landed[js, z] = final[js, 0]
            else:
                put("home", "home", final.at[js, s], landed.at[js, z], at(dz=SLOTS[s]))

    def flush():
        wait(("send", "spread"), amps.at[pl.ds(0, 6 * ROWS), pl.ds(0, PAIR)])
        wait(("send", "ring"), amps.at[pl.ds(0, 7 * SLOT_ROWS), :])
        for j in range(CHUNKS):
            wait(("send", ("b", j)), ints.at[j, pl.ds(0, 7 * HALF), :])
        for p, (j0, j1, s0, s1) in PASSES.items():
            js, ss = pl.ds(j0, j1 - j0), pl.ds(s0, s1 - s0)
            wait(("send", ("p", p)), second.at[js, :, ss])
            wait(("send", ("q", p)), first.at[js, :, ss])
        wait(("send", "home"), final.at[:, pl.ds(1, NZ - 1)])

    for event in ORDER:
        kind, rest = event[0], event[1:]
        if kind == "S":
            event_s(int(rest))
        elif kind == "A":
            event_a(int(rest[0]), int(rest[1]))
        elif kind == "B":
            event_b(int(rest[0]), int(rest[1]))
        elif kind == "P":
            event_p(rest)
        elif kind == "Q":
            event_q(rest)
        else:
            event_r(rest)

    wait("home", final.at[:, pl.ds(1, NZ - 1)])
    for zz in range(NZ):
        for j in range(CHUNKS):
            for half in range(2):
                o_ref[:, pl.ds(zz * PAIR + half * BLOCK + j * LANES, LANES)] = landed[j, zz, :, pl.ds(half * LANES, LANES)]
    flush()
    assert len(names) == SEMS, len(names)


def body(amplitudes, integrals):
    return pl.pallas_call(
        kernel,
        out_shape=jax.ShapeDtypeStruct((ROWS, NZ * PAIR), BF16),
        in_specs=[pl.BlockSpec(memory_space=pl.ANY)] * 2,
        out_specs=pl.BlockSpec(memory_space=pltpu.VMEM),
        scratch_shapes=[
            pltpu.VMEM((NZ * SLOT_ROWS, DEEP), BF16),
            pltpu.VMEM((CHUNKS, DEEP, WIDE), BF16),
            pltpu.VMEM((CHUNKS, NZ, NY, ROWS, WIDE), F32),
            pltpu.VMEM((CHUNKS, 2, NZ, ROWS, LANES), F32),
            pltpu.VMEM((CHUNKS, 2, NZ, ROWS, WIDE), F32),
            pltpu.VMEM((CHUNKS, NZ, ROWS, WIDE), BF16),
            pltpu.VMEM((CHUNKS, NZ, ROWS, WIDE), BF16),
            pltpu.SemaphoreType.DMA((SEMS,)),
        ],
        compiler_params=pltpu.CompilerParams(collective_id=0, has_side_effects=True, vmem_limit_bytes=56 << 20),
        cost_estimate=pl.CostEstimate(flops=2 * 512 * DEEP * PAIR, bytes_accessed=4 << 20, transcendentals=0),
    )(amplitudes, integrals)


def solution(mesh):
    return jax.shard_map(
        body,
        mesh=mesh,
        in_specs=(P(("col", "row"), None), P("col", "row")),
        out_specs=P(("col", "row"), None),
        check_vma=False,
    )
```

```python
import functools

import jax
import jax.numpy as jnp
from jax import lax
from jax.experimental import pallas as pl
from jax.experimental.pallas import tpu as pltpu
from jax.sharding import PartitionSpec as P

MESH = pl.DeviceIdType.MESH
BF16, F32 = jnp.bfloat16, jnp.float32

NX, NY, NZ = 4, 4, 8
ROWS = 16
BLOCK = 896
HALF = BLOCK // 2
LANES = 128
CHUNKS = BLOCK // LANES
WIDE = 2 * LANES
PAIR = 2 * BLOCK
DEEP = 4 * BLOCK
SLOTS = (0, 1, -1, 2, -2, 3, -3, 4)
SLOT_OF = {d: s for s, d in enumerate(SLOTS)}
SLOT_ROWS = NY * ROWS
SEMS = 77
SENDS = {
    None: ((0, 0), (0, 1), (1, 0)),
    0: ((1, 1), (2, 0)),
    1: ((2, 1), (3, 0)),
    2: ((3, 1), (4, 0)),
    3: ((4, 1), (5, 0)),
    4: ((5, 1),),
    5: ((6, 0), (6, 1)),
    6: (),
}

PASSES = {
    "a": (0, 1, 0, 3),
    "b": (1, 2, 0, 3),
    "c": (0, 2, 3, 5),
    "d": (2, 3, 0, 5),
    "e": (0, 3, 5, 7),
    "f": (3, 4, 0, 7),
    "g": (0, 4, 7, 8),
    "h": (4, 5, 0, 8),
    "i": (5, 6, 0, 8),
}
LAST = CHUNKS - 1

ORDER = (
    "S1", "S3", "B00", "S2", "A10", "B01", "A11", "B10", "A13", "B02", "A12", "B03", "Pa", "B11", "A20", "B20",
    "A21", "B12", "A23", "B13", "Pb", "B21", "Qa", "A22", "B30", "Pc", "A30", "B22", "Qb", "Ra", "A31", "B23",
    "Pd", "B31", "Qc", "A33", "B40", "Rb", "A32", "Pe", "B32", "Qd", "B33", "Pf", "B41", "Rc", "A40", "Qe",
    "B50", "Pg", "B42", "Rd", "B43", "Ph", "B51", "Qf", "B52", "Qg", "B53", "Qh", "B60", "Pi", "Re", "B61",
    "Rf", "PO", "B62", "Qi", "B63", "PF", "Rg", "Rh", "RO1", "RO0", "RF1", "Ri", "RF0",
)


def kernel(a_ref, b_ref, o_ref, amps, ints, part, first, second, final, landed, rest, sems):
    row, col = lax.axis_index("row"), lax.axis_index("col")
    z, x = row // 2, (row % 2) * 2 + col // 8
    y, core = (col // 2) % NY, col % 2

    def at(dx=0, dy=0, dz=0, dk=0):
        xx, yy, zz, kk = (x + dx) % NX, (y + dy) % NY, (z + dz) % NZ, (core + dk) % 2
        return (zz * 2 + xx // 2, (xx % 2) * 8 + yy * 2 + kk)

    names = {}

    def sem(name):
        return names.setdefault(name, len(names))

    def put(send, recv, src, dst, to):
        pltpu.make_async_remote_copy(
            src_ref=src, dst_ref=dst, send_sem=sems.at[sem(("send", send))], recv_sem=sems.at[sem(recv)],
            device_id=to, device_id_type=MESH,
        ).start()

    def wait(name, like):
        pltpu.make_async_copy(like, like, sems.at[sem(name)]).wait()

    def place(j, dx, dk, r0, n):
        xx, kk = (x + dx) % NX, (core + dk) % 2
        rows = pl.multiple_of(((xx % 2) * 2 + kk) * BLOCK + r0, 16)
        return ints.at[j, pl.ds(rows, n), pl.ds(pl.multiple_of((xx // 2) * LANES, LANES), LANES)]

    for h in range(2):
        pltpu.make_async_copy(
            a_ref.at[:, pl.ds(pl.multiple_of(h * 4 * PAIR + y * PAIR, LANES), PAIR)],
            amps.at[pl.ds(pl.multiple_of(y * ROWS, ROWS), ROWS), pl.ds(h * PAIR, PAIR)],
            sems.at[sem("own a")],
        ).start()
    for j in range(CHUNKS):
        pltpu.make_async_copy(b_ref.at[:, pl.ds(j * LANES, LANES)], place(j, 0, 0, 0, BLOCK), sems.at[sem("own b")]).start()

    partners = [at(dx=1), at(dx=-1), at(dk=1)]
    partners += [at(dy=d) for d in range(1, NY)] + [at(dz=d) for d in range(1, NZ)]
    barrier = pltpu.get_barrier_semaphore()
    for to in partners:
        pl.semaphore_signal(barrier, inc=1, device_id=to, device_id_type=MESH)
    pl.semaphore_wait(barrier, len(partners))

    def rows_of(d, dy):
        return pl.ds(pl.multiple_of(SLOT_OF[d] * SLOT_ROWS + (y + dy) % NY * ROWS, ROWS), ROWS)

    def hand_on(d, q):
        if d < 3 or q < 2:
            put("ring", ("ring", d + 1, q if d < 3 else 0), amps.at[rows_of(d, q), :], amps.at[rows_of(d + 1, q), :], at(dz=-1))
        if d < 3 or q >= 2:
            put("ring", ("ring", d + 1, q if d < 3 else 0), amps.at[rows_of(-d, q), :], amps.at[rows_of(4 if d == 3 else -(d + 1), q), :], at(dz=1))

    wait("own a", amps.at[pl.ds(0, ROWS), :])
    hand_on(0, 0)

    for d in (1, 3, 2):
        yy = (y + d) % NY
        for h in range(2):
            put(
                "spread",
                ("spread", NY - d),
                a_ref.at[:, pl.ds(pl.multiple_of(h * 4 * PAIR + yy * PAIR, LANES), PAIR)],
                amps.at[rows_of(0, 0), pl.ds(h * PAIR, PAIR)],
                at(dy=d),
            )

    def direct(j, step):
        for dx, r0 in ((1, step * HALF), (-1, (1 - step) * HALF)):
            put(
                "b", ("direct", j, step),
                b_ref.at[pl.ds(r0, HALF), pl.ds(j * LANES, LANES)], place(j, 0, 0, r0, HALF), at(dx=dx),
            )
        if step == 1:
            put("b", ("twin", j), b_ref.at[:, pl.ds(j * LANES, LANES)], place(j, 0, 0, 0, BLOCK), at(dk=1))

    for half in SENDS[None]:
        direct(*half)

    def event_s(q):
        wait(("spread", q), amps.at[pl.ds(0, ROWS), :])
        hand_on(0, q)

    def event_a(d, q):
        wait(("ring", d, q), amps.at[pl.ds(0, (4 if d == 4 else 2) * ROWS), :])
        if d < 4:
            hand_on(d, q)

    def event_b(j, step):
        two = ints.at[j, pl.ds(0, BLOCK), pl.ds(0, LANES)]
        if step == 0:
            wait(("direct", j, 0), two)
            for dx, r0 in ((1, 0), (-1, HALF)):
                put("b", ("onward", j), place(j, -dx, 0, r0, HALF), place(j, -dx, 0, r0, HALF), at(dx=dx))
            for half in SENDS[j]:
                direct(*half)
        elif step == 3:
            if j == 0:
                wait("own b", b_ref)
            if j == LAST:
                wait(("twin", j, "last"), two)
            else:
                wait(("twin", j), ints.at[j, :, pl.ds(0, LANES)])
        elif step == 1:
            wait(("direct", j, 1), two)
            for dx in (-1, 1):
                put("b", ("twin", j), place(j, dx, 0, 0, BLOCK), place(j, dx, 0, 0, BLOCK), at(dk=1))
        else:
            wait(("onward", j), two)
            name = ("twin", j, "last") if j == LAST else ("twin", j)
            put("b", name, place(j, 2, 0, 0, BLOCK), place(j, 2, 0, 0, BLOCK), at(dk=1))

    up, down, over = (y + 1) % NY, (y - 1) % NY, (y + 2) % NY
    LOW, HIGH = pl.ds(0, LANES), pl.ds(LANES, LANES)

    def event_p(p):
        j0, j1, s0, s1 = PASSES[p]
        js, ss = pl.ds(j0, j1 - j0), pl.ds(s0, s1 - s0)

        def one(j, carry):
            for m0, m1 in ((s0, s1),) if s1 - s0 < NZ else ((0, NZ // 2), (NZ // 2, NZ)):
                product = jnp.dot(amps[pl.ds(m0 * SLOT_ROWS, (m1 - m0) * SLOT_ROWS)], ints[j], preferred_element_type=F32)
                part[j, pl.ds(m0, m1 - m0)] = product.reshape(m1 - m0, NY, ROWS, WIDE)
            return carry

        if j1 - j0 == 1:
            one(j0, 0)
        else:
            lax.fori_loop(j0, j1, one, 0)
        put("p", ("far", p), part.at[js, ss, over, :, LOW], first.at[js, 0, ss], at(dy=1))
        put("p", ("far", p), part.at[js, ss, over, :, HIGH], first.at[js, 1, ss], at(dy=-1))
        put("p", ("near", p), part.at[js, ss, up, :, HIGH], second.at[js, 0, ss, :, HIGH], at(dy=1))
        put("p", ("near", p), part.at[js, ss, down, :, LOW], second.at[js, 1, ss, :, LOW], at(dy=-1))

    def event_q(p):
        j0, j1, s0, s1 = PASSES[p]
        js, ss = pl.ds(j0, j1 - j0), pl.ds(s0, s1 - s0)
        wait(("far", p), first.at[js, :, ss])
        first[js, 0, ss] += part[js, ss, up, :, LOW]
        put("q", ("near", p), first.at[js, 0, ss], second.at[js, 0, ss, :, LOW], at(dy=1))
        first[js, 1, ss] += part[js, ss, down, :, HIGH]
        put("q", ("near", p), first.at[js, 1, ss], second.at[js, 1, ss, :, HIGH], at(dy=-1))

    def event_r(p):
        j0, j1, s0, s1 = PASSES[p]
        js, ss = pl.ds(j0, j1 - j0), pl.ds(s0, s1 - s0)
        wait(("near", p), second.at[js, :, ss])
        total = part[js, ss, y] + second[js, 0, ss] + second[js, 1, ss]
        final[js, ss] = total.astype(BF16)
        for s in sorted(range(s0, s1), key=lambda s: -abs(SLOTS[s])):
            if s == 0:
                landed[js, z] = final[js, 0]
            else:
                put("home", "home", final.at[js, s], landed.at[js, z], at(dz=SLOTS[s]))

    def lane(own):
        return pl.ds(pl.multiple_of((x // 2 if own else 1 - x // 2) * LANES, LANES), LANES)

    def deep(near):
        return pl.ds(pl.multiple_of((1 - x % 2 if near else x % 2) * PAIR, LANES), PAIR)

    def share(ss, k, lanes, width):
        rows = pl.ds(ss.start * SLOT_ROWS, ss.size * SLOT_ROWS)
        product = jnp.dot(amps[rows, k], ints[LAST, k, lanes], preferred_element_type=F32)
        return product.reshape(ss.size, NY, ROWS, width)

    halves = (pl.ds(0, NZ // 2), pl.ds(NZ // 2, NZ // 2))

    def last_p(own, k):
        here = lane(own)
        for half in (1, 0):
            ss = halves[half]
            part[LAST, ss, :, :, here] += share(ss, k, here, LANES)
            for d in (2, 1, 3):
                put("rest", ("rest", own, half), part.at[LAST, ss, (y + d) % NY, :, here], rest.at[int(own), d - 1, ss], at(dy=d))

    def last_r(own, half):
        here, ss, o = lane(own), halves[half], int(own)
        wait(("rest", own, half), rest.at[o, :, ss])
        total = part[LAST, ss, y, :, here] + rest[o, 0, ss] + rest[o, 1, ss] + rest[o, 2, ss]
        final[LAST, ss, :, here] = total.astype(BF16)
        for s in range(ss.start + ss.size - 1, max(ss.start, 1) - 1, -1):
            put("home", "home", final.at[LAST, s, :, here], landed.at[LAST, z, :, here], at(dz=SLOTS[s]))
        if half == 0:
            landed[LAST, z, :, here] = final[LAST, 0, :, here]

    def own_p():
        wait(("twin", LAST), ints.at[LAST, pl.ds(0, 3 * BLOCK), pl.ds(0, LANES)])
        for ss in halves:
            part[LAST, ss] = share(ss, deep(True), pl.ds(0, WIDE), WIDE)
        last_p(True, deep(False))

    def flush():
        wait(("send", "spread"), amps.at[pl.ds(0, 6 * ROWS), pl.ds(0, PAIR)])
        wait(("send", "ring"), amps.at[pl.ds(0, 7 * SLOT_ROWS), :])
        wait(("send", "b"), ints.at[:, pl.ds(0, 7 * HALF), :])
        wait(("send", "p"), second)
        wait(("send", "q"), first)
        wait(("send", "rest"), rest)
        wait(("send", "home"), final.at[:, pl.ds(1, NZ - 1)])

    ends = {"PO": own_p, "PF": functools.partial(last_p, False, deep(False))}
    ends |= {f"R{c}{half}": functools.partial(last_r, c == "O", half) for c in "OF" for half in range(2)}
    for event in ORDER:
        kind, which = event[0], event[1:]
        if kind == "S":
            event_s(int(which))
        elif kind == "A":
            event_a(int(which[0]), int(which[1]))
        elif kind == "B":
            event_b(int(which[0]), int(which[1]))
        elif event in ends:
            ends[event]()
        elif kind == "P":
            event_p(which)
        elif kind == "Q":
            event_q(which)
        else:
            event_r(which)

    wait("home", final.at[:, pl.ds(1, NZ - 1)])
    for zz in range(NZ):
        for j in range(CHUNKS):
            for half in range(2):
                o_ref[:, pl.ds(zz * PAIR + half * BLOCK + j * LANES, LANES)] = landed[j, zz, :, pl.ds(half * LANES, LANES)]
    flush()
    assert len(names) == SEMS, len(names)


def body(amplitudes, integrals):
    return pl.pallas_call(
        kernel,
        out_shape=jax.ShapeDtypeStruct((ROWS, NZ * PAIR), BF16),
        in_specs=[pl.BlockSpec(memory_space=pl.ANY)] * 2,
        out_specs=pl.BlockSpec(memory_space=pltpu.VMEM),
        scratch_shapes=[
            pltpu.VMEM((NZ * SLOT_ROWS, DEEP), BF16),
            pltpu.VMEM((CHUNKS, DEEP, WIDE), BF16),
            pltpu.VMEM((CHUNKS, NZ, NY, ROWS, WIDE), F32),
            pltpu.VMEM((LAST, 2, NZ, ROWS, LANES), F32),
            pltpu.VMEM((LAST, 2, NZ, ROWS, WIDE), F32),
            pltpu.VMEM((CHUNKS, NZ, ROWS, WIDE), BF16),
            pltpu.VMEM((CHUNKS, NZ, ROWS, WIDE), BF16),
            pltpu.VMEM((2, NY - 1, NZ, ROWS, LANES), F32),
            pltpu.SemaphoreType.DMA((SEMS,)),
        ],
        compiler_params=pltpu.CompilerParams(collective_id=0, has_side_effects=True, vmem_limit_bytes=56 << 20),
        cost_estimate=pl.CostEstimate(flops=2 * 512 * DEEP * PAIR, bytes_accessed=4 << 20, transcendentals=0),
    )(amplitudes, integrals)


def solution(mesh):
    return jax.shard_map(
        body,
        mesh=mesh,
        in_specs=(P(("col", "row"), None), P("col", "row")),
        out_specs=P(("col", "row"), None),
        check_vma=False,
    )
```

```python
import functools

import jax
import jax.numpy as jnp
from jax import lax
from jax.experimental import pallas as pl
from jax.experimental.pallas import tpu as pltpu
from jax.sharding import PartitionSpec as P

MESH = pl.DeviceIdType.MESH
BF16, F32 = jnp.bfloat16, jnp.float32

NX, NY, NZ = 4, 4, 8
ROWS = 16
BLOCK = 896
HALF = BLOCK // 2
LANES = 128
CHUNKS = BLOCK // LANES
WIDE = 2 * LANES
PAIR = 2 * BLOCK
DEEP = 4 * BLOCK
SLOTS = (0, 1, -1, 2, -2, 3, -3, 4)
SLOT_OF = {d: s for s, d in enumerate(SLOTS)}
SLOT_ROWS = NY * ROWS
SEMS = 83
SENDS = {
    None: ((0, 0), (0, 1), (1, 0)),
    0: ((1, 1), (2, 0)),
    1: ((2, 1), (3, 0)),
    2: ((3, 1), (4, 0)),
    3: ((4, 1), (5, 0)),
    4: ((5, 1),),
    5: ((6, 0), (6, 1)),
    6: (),
}

PASSES = {
    "a": (0, 1, 0, 3),
    "b": (1, 2, 0, 3),
    "c": (0, 2, 3, 5),
    "d": (2, 3, 0, 5),
    "e": (0, 3, 5, 7),
    "f": (3, 4, 0, 7),
    "g": (0, 4, 7, 8),
}
LAST = CHUNKS - 1
SPLIT = (4, 5, LAST)

ORDER = (
    "S1", "S3", "B00", "S2", "A10", "B01", "A11", "B10", "A13", "B02", "A12", "B03", "Pa", "B11", "A20", "B20",
    "A21", "B12", "A23", "B13", "Pb", "B21", "Qa", "A22", "B30", "Pc", "A30", "B22", "Qb", "Ra", "A31", "B23",
    "Pd", "B31", "Qc", "A33", "B40", "Rb", "A32", "Pe", "B32", "Qd", "B33", "Pf", "B41", "A40", "Qe", "B50",
    "O4P", "Rc", "Pg", "B42", "Rd", "B43", "F4P", "B51", "Qf", "O4Q", "B52", "Qg", "O5P", "B60", "B53", "F5P",
    "F4Q", "B61", "Re", "O5Q", "O6P", "B62", "O4R", "F5Q", "B63", "F6P", "Rf", "Rg", "F4R", "O5R", "O6R", "O6S",
    "F5R", "F6R", "F6S",
)


def kernel(a_ref, b_ref, o_ref, amps, ints, part, first, second, final, landed, rest, sems):
    row, col = lax.axis_index("row"), lax.axis_index("col")
    z, x = row // 2, (row % 2) * 2 + col // 8
    y, core = (col // 2) % NY, col % 2

    def at(dx=0, dy=0, dz=0, dk=0):
        xx, yy, zz, kk = (x + dx) % NX, (y + dy) % NY, (z + dz) % NZ, (core + dk) % 2
        return (zz * 2 + xx // 2, (xx % 2) * 8 + yy * 2 + kk)

    names = {}

    def sem(name):
        return names.setdefault(name, len(names))

    def put(send, recv, src, dst, to):
        pltpu.make_async_remote_copy(
            src_ref=src, dst_ref=dst, send_sem=sems.at[sem(("send", send))], recv_sem=sems.at[sem(recv)],
            device_id=to, device_id_type=MESH,
        ).start()

    def wait(name, like):
        pltpu.make_async_copy(like, like, sems.at[sem(name)]).wait()

    def place(j, dx, dk, r0, n):
        xx, kk = (x + dx) % NX, (core + dk) % 2
        rows = pl.multiple_of(((xx % 2) * 2 + kk) * BLOCK + r0, 16)
        return ints.at[j, pl.ds(rows, n), pl.ds(pl.multiple_of((xx // 2) * LANES, LANES), LANES)]

    for h in range(2):
        pltpu.make_async_copy(
            a_ref.at[:, pl.ds(pl.multiple_of(h * 4 * PAIR + y * PAIR, LANES), PAIR)],
            amps.at[pl.ds(pl.multiple_of(y * ROWS, ROWS), ROWS), pl.ds(h * PAIR, PAIR)],
            sems.at[sem("own a")],
        ).start()
    for j in range(CHUNKS):
        pltpu.make_async_copy(b_ref.at[:, pl.ds(j * LANES, LANES)], place(j, 0, 0, 0, BLOCK), sems.at[sem("own b")]).start()

    partners = [at(dx=1), at(dx=-1), at(dk=1)]
    partners += [at(dy=d) for d in range(1, NY)] + [at(dz=1), at(dz=-1)]
    barrier = pltpu.get_barrier_semaphore()
    for to in partners:
        pl.semaphore_signal(barrier, inc=1, device_id=to, device_id_type=MESH)
    pl.semaphore_wait(barrier, len(partners))

    def rows_of(d, dy):
        return pl.ds(pl.multiple_of(SLOT_OF[d] * SLOT_ROWS + (y + dy) % NY * ROWS, ROWS), ROWS)

    def hand_on(d, q):
        if d < 3 or q < 2:
            put("ring", ("ring", d + 1, q if d < 3 else 0), amps.at[rows_of(d, q), :], amps.at[rows_of(d + 1, q), :], at(dz=-1))
        if d < 3 or q >= 2:
            put("ring", ("ring", d + 1, q if d < 3 else 0), amps.at[rows_of(-d, q), :], amps.at[rows_of(4 if d == 3 else -(d + 1), q), :], at(dz=1))

    wait("own a", amps.at[pl.ds(0, ROWS), :])
    hand_on(0, 0)

    for d in (1, 3, 2):
        yy = (y + d) % NY
        for h in range(2):
            put(
                "spread",
                ("spread", NY - d),
                a_ref.at[:, pl.ds(pl.multiple_of(h * 4 * PAIR + yy * PAIR, LANES), PAIR)],
                amps.at[rows_of(0, 0), pl.ds(h * PAIR, PAIR)],
                at(dy=d),
            )

    def direct(j, step):
        for dx, r0 in ((1, step * HALF), (-1, (1 - step) * HALF)):
            put(
                "b", ("direct", j, step),
                b_ref.at[pl.ds(r0, HALF), pl.ds(j * LANES, LANES)], place(j, 0, 0, r0, HALF), at(dx=dx),
            )
        if step == 1:
            put("b", ("twin", j), b_ref.at[:, pl.ds(j * LANES, LANES)], place(j, 0, 0, 0, BLOCK), at(dk=1))

    for half in SENDS[None]:
        direct(*half)

    def event_s(q):
        wait(("spread", q), amps.at[pl.ds(0, ROWS), :])
        hand_on(0, q)

    def event_a(d, q):
        wait(("ring", d, q), amps.at[pl.ds(0, (4 if d == 4 else 2) * ROWS), :])
        if d < 4:
            hand_on(d, q)

    def event_b(j, step):
        two = ints.at[j, pl.ds(0, BLOCK), pl.ds(0, LANES)]
        if step == 0:
            wait(("direct", j, 0), two)
            for dx, r0 in ((1, 0), (-1, HALF)):
                put("b", ("onward", j), place(j, -dx, 0, r0, HALF), place(j, -dx, 0, r0, HALF), at(dx=dx))
            for half in SENDS[j]:
                direct(*half)
        elif step == 3:
            if j == 0:
                wait("own b", b_ref)
            if j in SPLIT:
                wait(("twin", j, "last"), two)
            else:
                wait(("twin", j), ints.at[j, :, pl.ds(0, LANES)])
        elif step == 1:
            wait(("direct", j, 1), two)
            for dx in (-1, 1):
                put("b", ("twin", j), place(j, dx, 0, 0, BLOCK), place(j, dx, 0, 0, BLOCK), at(dk=1))
        else:
            wait(("onward", j), two)
            name = ("twin", j, "last") if j in SPLIT else ("twin", j)
            put("b", name, place(j, 2, 0, 0, BLOCK), place(j, 2, 0, 0, BLOCK), at(dk=1))

    up, down, over = (y + 1) % NY, (y - 1) % NY, (y + 2) % NY
    LOW, HIGH = pl.ds(0, LANES), pl.ds(LANES, LANES)

    def event_p(p):
        j0, j1, s0, s1 = PASSES[p]
        js, ss = pl.ds(j0, j1 - j0), pl.ds(s0, s1 - s0)

        def one(j, carry):
            for m0, m1 in ((s0, s1),) if s1 - s0 < 6 else ((s0, NZ // 2), (NZ // 2, s1)):
                product = jnp.dot(amps[pl.ds(m0 * SLOT_ROWS, (m1 - m0) * SLOT_ROWS)], ints[j], preferred_element_type=F32)
                part[j, pl.ds(m0, m1 - m0)] = product.reshape(m1 - m0, NY, ROWS, WIDE)
            return carry

        if j1 - j0 == 1:
            one(j0, 0)
        else:
            lax.fori_loop(j0, j1, one, 0)
        put("p", ("far", p), part.at[js, ss, over, :, LOW], first.at[js, 0, ss], at(dy=1))
        put("p", ("far", p), part.at[js, ss, over, :, HIGH], first.at[js, 1, ss], at(dy=-1))
        put("p", ("near", p), part.at[js, ss, up, :, HIGH], second.at[js, 0, ss, :, HIGH], at(dy=1))
        put("p", ("near", p), part.at[js, ss, down, :, LOW], second.at[js, 1, ss, :, LOW], at(dy=-1))

    def event_q(p):
        j0, j1, s0, s1 = PASSES[p]
        js, ss = pl.ds(j0, j1 - j0), pl.ds(s0, s1 - s0)
        wait(("far", p), first.at[js, :, ss])
        first[js, 0, ss] += part[js, ss, up, :, LOW]
        put("q", ("near", p), first.at[js, 0, ss], second.at[js, 0, ss, :, LOW], at(dy=1))
        first[js, 1, ss] += part[js, ss, down, :, HIGH]
        put("q", ("near", p), first.at[js, 1, ss], second.at[js, 1, ss, :, HIGH], at(dy=-1))

    def event_r(p):
        j0, j1, s0, s1 = PASSES[p]
        js, ss = pl.ds(j0, j1 - j0), pl.ds(s0, s1 - s0)
        wait(("near", p), second.at[js, :, ss])
        total = part[js, ss, y] + second[js, 0, ss] + second[js, 1, ss]
        final[js, ss] = total.astype(BF16)
        for s in sorted(range(s0, s1), key=lambda s: -abs(SLOTS[s])):
            if s == 0:
                landed[js, z] = final[js, 0]
            else:
                put("home", "home", final.at[js, s], landed.at[js, z], at(dz=SLOTS[s]))

    def lane(own):
        return pl.ds(pl.multiple_of((x // 2 if own else 1 - x // 2) * LANES, LANES), LANES)

    def deep(near):
        return pl.ds(pl.multiple_of((1 - x % 2 if near else x % 2) * PAIR, LANES), PAIR)

    def share(j, ss, k, lanes, width):
        rows = pl.ds(ss.start * SLOT_ROWS, ss.size * SLOT_ROWS)
        product = jnp.dot(amps[rows, k], ints[j, k, lanes], preferred_element_type=F32)
        return product.reshape(ss.size, NY, ROWS, width)

    halves = (pl.ds(0, NZ // 2), pl.ds(NZ // 2, NZ // 2))

    def own_products(j):
        wait(("twin", j), ints.at[j, pl.ds(0, 3 * BLOCK), pl.ds(0, LANES)])
        for ss in halves:
            part[j, ss] = share(j, ss, deep(True), pl.ds(0, WIDE), WIDE)

    def split_p(j, own):
        u, d = halves if own else halves[::-1]
        here = lane(own)
        if own:
            own_products(j)
        for ss in halves:
            part[j, ss, :, :, here] += share(j, ss, deep(False), here, LANES)
        put("p", ("far", j, own), part.at[j, u, over, :, here], first.at[j, 0, u], at(dy=1))
        put("p", ("far", j, own), part.at[j, d, over, :, here], first.at[j, 1, d], at(dy=-1))
        put("p", ("near", j, own), part.at[j, d, up, :, here], second.at[j, 0, d, :, here], at(dy=1))
        put("p", ("near", j, own), part.at[j, u, down, :, here], second.at[j, 1, u, :, here], at(dy=-1))

    def split_q(j, own):
        u, d = halves if own else halves[::-1]
        here = lane(own)
        wait(("far", j, own), first.at[j, 0])
        first[j, 0, u] += part[j, u, up, :, here]
        put("q", ("near", j, own), first.at[j, 0, u], second.at[j, 0, u, :, here], at(dy=1))
        first[j, 1, d] += part[j, d, down, :, here]
        put("q", ("near", j, own), first.at[j, 1, d], second.at[j, 1, d, :, here], at(dy=-1))

    def settle(j, ss, here, total):
        final[j, ss, :, here] = total.astype(BF16)
        for s in range(ss.start + ss.size - 1, max(ss.start, 1) - 1, -1):
            put("home", "home", final.at[j, s, :, here], landed.at[j, z, :, here], at(dz=SLOTS[s]))
        if ss.start == 0:
            landed[j, z, :, here] = final[j, 0, :, here]

    def split_r(j, own):
        here = lane(own)
        wait(("near", j, own), second.at[j, 0])
        settle(j, pl.ds(0, NZ), here, part[j, :, y, :, here] + second[j, 0, :, :, here] + second[j, 1, :, :, here])

    def last_p(own):
        here = lane(own)
        if own:
            own_products(LAST)
        for half in (1, 0):
            ss = halves[half]
            part[LAST, ss, :, :, here] += share(LAST, ss, deep(False), here, LANES)
            for d in (2, 1, 3):
                put("rest", ("rest", own, half), part.at[LAST, ss, (y + d) % NY, :, here], rest.at[int(own), d - 1, ss], at(dy=d))

    def last_r(own, half):
        here, ss, o = lane(own), halves[half], int(own)
        wait(("rest", own, half), rest.at[o, :, ss])
        settle(LAST, ss, here, part[LAST, ss, y, :, here] + rest[o, 0, ss] + rest[o, 1, ss] + rest[o, 2, ss])

    homes = final.at[:, pl.ds(1, NZ - 1)]

    def flush():
        wait(("send", "spread"), amps.at[pl.ds(0, 6 * ROWS), pl.ds(0, PAIR)])
        wait(("send", "ring"), amps.at[pl.ds(0, 7 * SLOT_ROWS), :])
        wait(("send", "b"), ints.at[:, pl.ds(0, 7 * HALF), :])
        wait(("send", "p"), second)
        wait(("send", "q"), first)
        wait(("send", "rest"), rest)
        wait(("send", "home"), homes)

    ends = {}
    for part_of, own in (("O", True), ("F", False)):
        ends[f"{part_of}6P"] = functools.partial(last_p, own)
        ends[f"{part_of}6R"] = functools.partial(last_r, own, 1)
        ends[f"{part_of}6S"] = functools.partial(last_r, own, 0)
    for step, do in (("P", split_p), ("Q", split_q), ("R", split_r)):
        ends |= {f"O{j}{step}": functools.partial(do, j, True) for j in SPLIT[:-1]}
        ends |= {f"F{j}{step}": functools.partial(do, j, False) for j in SPLIT[:-1]}
    for event in ORDER:
        kind, which = event[0], event[1:]
        if event in ends:
            ends[event]()
        elif kind == "S":
            event_s(int(which))
        elif kind == "A":
            event_a(int(which[0]), int(which[1]))
        elif kind == "B":
            event_b(int(which[0]), int(which[1]))
        elif kind == "P":
            event_p(which)
        elif kind == "Q":
            event_q(which)
        else:
            event_r(which)

    wait("home", homes)
    for zz in range(NZ):
        for j in range(CHUNKS):
            for half in range(2):
                o_ref[:, pl.ds(zz * PAIR + half * BLOCK + j * LANES, LANES)] = landed[j, zz, :, pl.ds(half * LANES, LANES)]
    flush()
    assert len(names) == SEMS, len(names)


def body(amplitudes, integrals):
    return pl.pallas_call(
        kernel,
        out_shape=jax.ShapeDtypeStruct((ROWS, NZ * PAIR), BF16),
        in_specs=[pl.BlockSpec(memory_space=pl.ANY)] * 2,
        out_specs=pl.BlockSpec(memory_space=pltpu.VMEM),
        scratch_shapes=[
            pltpu.VMEM((NZ * SLOT_ROWS, DEEP), BF16),
            pltpu.VMEM((CHUNKS, DEEP, WIDE), BF16),
            pltpu.VMEM((CHUNKS, NZ, NY, ROWS, WIDE), F32),
            pltpu.VMEM((LAST, 2, NZ, ROWS, LANES), F32),
            pltpu.VMEM((LAST, 2, NZ, ROWS, WIDE), F32),
            pltpu.VMEM((CHUNKS, NZ, ROWS, WIDE), BF16),
            pltpu.VMEM((CHUNKS, NZ, ROWS, WIDE), BF16),
            pltpu.VMEM((2, NY - 1, NZ, ROWS, LANES), F32),
            pltpu.SemaphoreType.DMA((SEMS,)),
        ],
        compiler_params=pltpu.CompilerParams(collective_id=0, has_side_effects=True, vmem_limit_bytes=56 << 20),
        cost_estimate=pl.CostEstimate(flops=2 * 512 * DEEP * PAIR, bytes_accessed=4 << 20, transcendentals=0),
    )(amplitudes, integrals)


def solution(mesh):
    return jax.shard_map(
        body,
        mesh=mesh,
        in_specs=(P(("col", "row"), None), P("col", "row")),
        out_specs=P(("col", "row"), None),
        check_vma=False,
    )
```

```python
import functools

import jax
import jax.numpy as jnp
from jax import lax
from jax.experimental import pallas as pl
from jax.experimental.pallas import tpu as pltpu
from jax.sharding import PartitionSpec as P

MESH = pl.DeviceIdType.MESH
BF16, F32 = jnp.bfloat16, jnp.float32

NX, NY, NZ = 4, 4, 8
ROWS = 16
BLOCK = 896
HALF = BLOCK // 2
LANES = 128
CHUNKS = BLOCK // LANES
WIDE = 2 * LANES
PAIR = 2 * BLOCK
DEEP = 4 * BLOCK
SLOTS = (0, 1, -1, 2, -2, 3, -3, 4)
SLOT_OF = {d: s for s, d in enumerate(SLOTS)}
SLOT_ROWS = NY * ROWS
VMEM = 427 << 17
SEMS = 83
SENDS = {
    None: ((0, 0), (0, 1), (1, 0)),
    0: ((1, 1), (2, 0)),
    1: ((2, 1), (3, 0)),
    2: ((3, 1), (4, 0)),
    3: ((4, 1), (5, 0)),
    4: ((5, 1),),
    5: ((6, 0), (6, 1)),
    6: (),
}

PASSES = {
    "a": (0, 1, 0, 3),
    "b": (1, 2, 0, 3),
    "c": (0, 2, 3, 5),
    "d": (2, 3, 0, 5),
    "e": (0, 3, 5, 7),
    "f": (3, 4, 0, 7),
    "g": (0, 4, 7, 8),
}
LAST = CHUNKS - 1
SPLIT = (4, 5, LAST)

ORDER = (
    "S1", "S3", "B00", "S2", "A10", "B01", "A11", "B10", "A13", "B02", "A12", "B03", "Pa", "B11", "A20", "B20",
    "A21", "B12", "A23", "B13", "Pb", "B21", "Qa", "A22", "B30", "Pc", "A30", "B22", "Qb", "Ra", "A31", "B23",
    "Pd", "B31", "Qc", "A33", "B40", "Rb", "A32", "Pe", "B32", "Qd", "B33", "Pf", "B41", "A40", "Qe", "B50",
    "O4P", "Rc", "Pg", "B42", "Rd", "B43", "F4P", "B51", "Qf", "O4Q", "B52", "Qg", "O5P", "B60", "B53", "F5P",
    "F4Q", "B61", "Re", "O5Q", "O6P", "B62", "O4R", "F5Q", "B63", "F6P", "Rf", "Rg", "F4R", "O5R", "O6R", "O6S",
    "F5R", "F6R", "F6S",
)


def kernel(a_ref, b_ref, o_ref, amps, ints, part, first, second, final, landed, rest, sems):
    row, col = lax.axis_index("row"), lax.axis_index("col")
    z, x = row // 2, (row % 2) * 2 + col // 8
    y, core = (col // 2) % NY, col % 2

    def at(dx=0, dy=0, dz=0, dk=0):
        xx, yy, zz, kk = (x + dx) % NX, (y + dy) % NY, (z + dz) % NZ, (core + dk) % 2
        return (zz * 2 + xx // 2, (xx % 2) * 8 + yy * 2 + kk)

    names = {}

    def sem(name):
        return names.setdefault(name, len(names))

    def put(send, recv, src, dst, to):
        pltpu.make_async_remote_copy(
            src_ref=src, dst_ref=dst, send_sem=sems.at[sem(("send", send))], recv_sem=sems.at[sem(recv)],
            device_id=to, device_id_type=MESH,
        ).start()

    def wait(name, like):
        pltpu.make_async_copy(like, like, sems.at[sem(name)]).wait()

    def place(j, dx, dk, r0, n):
        xx, kk = (x + dx) % NX, (core + dk) % 2
        rows = pl.multiple_of(((xx % 2) * 2 + kk) * BLOCK + r0, 16)
        return ints.at[j, pl.ds(rows, n), pl.ds(pl.multiple_of((xx // 2) * LANES, LANES), LANES)]

    for h in range(2):
        pltpu.make_async_copy(
            a_ref.at[:, pl.ds(pl.multiple_of(h * 4 * PAIR + y * PAIR, LANES), PAIR)],
            amps.at[pl.ds(pl.multiple_of(y * ROWS, ROWS), ROWS), pl.ds(h * PAIR, PAIR)],
            sems.at[sem("own a")],
        ).start()
    for j in range(CHUNKS):
        pltpu.make_async_copy(b_ref.at[:, pl.ds(j * LANES, LANES)], place(j, 0, 0, 0, BLOCK), sems.at[sem("own b")]).start()

    partners = [at(dx=1), at(dx=-1), at(dk=1)]
    partners += [at(dy=d) for d in range(1, NY)] + [at(dz=1), at(dz=-1)]
    barrier = pltpu.get_barrier_semaphore()
    for to in partners:
        pl.semaphore_signal(barrier, inc=1, device_id=to, device_id_type=MESH)
    pl.semaphore_wait(barrier, len(partners))

    def rows_of(d, dy):
        return pl.ds(pl.multiple_of(SLOT_OF[d] * SLOT_ROWS + (y + dy) % NY * ROWS, ROWS), ROWS)

    def hand_on(d, q):
        if d < 3 or q < 2:
            put("ring", ("ring", d + 1, q if d < 3 else 0), amps.at[rows_of(d, q), :], amps.at[rows_of(d + 1, q), :], at(dz=-1))
        if d < 3 or q >= 2:
            put("ring", ("ring", d + 1, q if d < 3 else 0), amps.at[rows_of(-d, q), :], amps.at[rows_of(4 if d == 3 else -(d + 1), q), :], at(dz=1))

    wait("own a", amps.at[pl.ds(0, ROWS), :])
    hand_on(0, 0)

    for d in (1, 3, 2):
        yy = (y + d) % NY
        for h in range(2):
            put(
                "spread",
                ("spread", NY - d),
                a_ref.at[:, pl.ds(pl.multiple_of(h * 4 * PAIR + yy * PAIR, LANES), PAIR)],
                amps.at[rows_of(0, 0), pl.ds(h * PAIR, PAIR)],
                at(dy=d),
            )

    def direct(j, step):
        for dx, r0 in ((1, step * HALF), (-1, (1 - step) * HALF)):
            put(
                "b", ("direct", j, step),
                b_ref.at[pl.ds(r0, HALF), pl.ds(j * LANES, LANES)], place(j, 0, 0, r0, HALF), at(dx=dx),
            )
        if step == 1:
            put("b", ("twin", j), b_ref.at[:, pl.ds(j * LANES, LANES)], place(j, 0, 0, 0, BLOCK), at(dk=1))

    for half in SENDS[None]:
        direct(*half)

    def event_s(q):
        wait(("spread", q), amps.at[pl.ds(0, ROWS), :])
        hand_on(0, q)

    def event_a(d, q):
        wait(("ring", d, q), amps.at[pl.ds(0, (4 if d == 4 else 2) * ROWS), :])
        if d < 4:
            hand_on(d, q)

    def event_b(j, step):
        two = ints.at[j, pl.ds(0, BLOCK), pl.ds(0, LANES)]
        if step == 0:
            wait(("direct", j, 0), two)
            for dx, r0 in ((1, 0), (-1, HALF)):
                put("b", ("onward", j), place(j, -dx, 0, r0, HALF), place(j, -dx, 0, r0, HALF), at(dx=dx))
            for half in SENDS[j]:
                direct(*half)
        elif step == 3:
            if j == 0:
                wait("own b", b_ref)
            if j in SPLIT:
                wait(("twin", j, "last"), two)
            else:
                wait(("twin", j), ints.at[j, :, pl.ds(0, LANES)])
        elif step == 1:
            wait(("direct", j, 1), two)
            for dx in (-1, 1):
                put("b", ("twin", j), place(j, dx, 0, 0, BLOCK), place(j, dx, 0, 0, BLOCK), at(dk=1))
        else:
            wait(("onward", j), two)
            name = ("twin", j, "last") if j in SPLIT else ("twin", j)
            put("b", name, place(j, 2, 0, 0, BLOCK), place(j, 2, 0, 0, BLOCK), at(dk=1))

    up, down, over = (y + 1) % NY, (y - 1) % NY, (y + 2) % NY
    LOW, HIGH = pl.ds(0, LANES), pl.ds(LANES, LANES)

    def event_p(p):
        j0, j1, s0, s1 = PASSES[p]
        js, ss = pl.ds(j0, j1 - j0), pl.ds(s0, s1 - s0)

        def one(j, carry):
            for m0, m1 in ((s0, s1),) if s1 - s0 < 6 else ((s0, NZ // 2), (NZ // 2, s1)):
                product = jnp.dot(amps[pl.ds(m0 * SLOT_ROWS, (m1 - m0) * SLOT_ROWS)], ints[j], preferred_element_type=F32)
                part[j, pl.ds(m0, m1 - m0)] = product.reshape(m1 - m0, NY, ROWS, WIDE)
            return carry

        if j1 - j0 == 1:
            one(j0, 0)
        else:
            lax.fori_loop(j0, j1, one, 0)
        put("p", ("far", p), part.at[js, ss, over, :, LOW], first.at[js, 0, ss], at(dy=1))
        put("p", ("far", p), part.at[js, ss, over, :, HIGH], first.at[js, 1, ss], at(dy=-1))
        put("p", ("near", p), part.at[js, ss, up, :, HIGH], second.at[js, 0, ss, :, HIGH], at(dy=1))
        put("p", ("near", p), part.at[js, ss, down, :, LOW], second.at[js, 1, ss, :, LOW], at(dy=-1))

    def event_q(p):
        j0, j1, s0, s1 = PASSES[p]
        js, ss = pl.ds(j0, j1 - j0), pl.ds(s0, s1 - s0)
        wait(("far", p), first.at[js, :, ss])
        first[js, 0, ss] += part[js, ss, up, :, LOW]
        put("q", ("near", p), first.at[js, 0, ss], second.at[js, 0, ss, :, LOW], at(dy=1))
        first[js, 1, ss] += part[js, ss, down, :, HIGH]
        put("q", ("near", p), first.at[js, 1, ss], second.at[js, 1, ss, :, HIGH], at(dy=-1))

    def event_r(p):
        j0, j1, s0, s1 = PASSES[p]
        js, ss = pl.ds(j0, j1 - j0), pl.ds(s0, s1 - s0)
        wait(("near", p), second.at[js, :, ss])
        total = part[js, ss, y] + second[js, 0, ss] + second[js, 1, ss]
        final[js, ss] = total.astype(BF16)
        for s in sorted(range(s0, s1), key=lambda s: -abs(SLOTS[s])):
            if s == 0:
                landed[js, z] = final[js, 0]
            else:
                put("home", "home", final.at[js, s], landed.at[js, z], at(dz=SLOTS[s]))

    def lane(own):
        return pl.ds(pl.multiple_of((x // 2 if own else 1 - x // 2) * LANES, LANES), LANES)

    def deep(near):
        return pl.ds(pl.multiple_of((1 - x % 2 if near else x % 2) * PAIR, LANES), PAIR)

    def share(j, ss, k, lanes, width):
        rows = pl.ds(ss.start * SLOT_ROWS, ss.size * SLOT_ROWS)
        product = jnp.dot(amps[rows, k], ints[j, k, lanes], preferred_element_type=F32)
        return product.reshape(ss.size, NY, ROWS, width)

    halves = (pl.ds(0, NZ // 2), pl.ds(NZ // 2, NZ // 2))

    def own_products(j):
        wait(("twin", j), ints.at[j, pl.ds(0, 3 * BLOCK), pl.ds(0, LANES)])
        for ss in halves:
            part[j, ss] = share(j, ss, deep(True), pl.ds(0, WIDE), WIDE)

    def split_p(j, own):
        u, d = halves if own else halves[::-1]
        here = lane(own)
        if own:
            own_products(j)
        for ss in halves:
            part[j, ss, :, :, here] += share(j, ss, deep(False), here, LANES)
        put("p", ("far", j, own), part.at[j, u, over, :, here], first.at[j, 0, u], at(dy=1))
        put("p", ("far", j, own), part.at[j, d, over, :, here], first.at[j, 1, d], at(dy=-1))
        put("p", ("near", j, own), part.at[j, d, up, :, here], second.at[j, 0, d, :, here], at(dy=1))
        put("p", ("near", j, own), part.at[j, u, down, :, here], second.at[j, 1, u, :, here], at(dy=-1))

    def split_q(j, own):
        u, d = halves if own else halves[::-1]
        here = lane(own)
        wait(("far", j, own), first.at[j, 0])
        first[j, 0, u] += part[j, u, up, :, here]
        put("q", ("near", j, own), first.at[j, 0, u], second.at[j, 0, u, :, here], at(dy=1))
        first[j, 1, d] += part[j, d, down, :, here]
        put("q", ("near", j, own), first.at[j, 1, d], second.at[j, 1, d, :, here], at(dy=-1))

    def settle(j, ss, here, total):
        final[j, ss, :, here] = total.astype(BF16)
        for s in range(ss.start + ss.size - 1, max(ss.start, 1) - 1, -1):
            put("home", "home", final.at[j, s, :, here], landed.at[j, z, :, here], at(dz=SLOTS[s]))
        if ss.start == 0:
            landed[j, z, :, here] = final[j, 0, :, here]

    def split_r(j, own):
        here = lane(own)
        wait(("near", j, own), second.at[j, 0])
        settle(j, pl.ds(0, NZ), here, part[j, :, y, :, here] + second[j, 0, :, :, here] + second[j, 1, :, :, here])

    def last_p(own):
        here = lane(own)
        if own:
            own_products(LAST)
        for half in (1, 0):
            ss = halves[half]
            part[LAST, ss, :, :, here] += share(LAST, ss, deep(False), here, LANES)
            for d in (2, 1, 3):
                put("rest", ("rest", own, half), part.at[LAST, ss, (y + d) % NY, :, here], rest.at[int(own), d - 1, ss], at(dy=d))

    def last_r(own, half):
        here, ss, o = lane(own), halves[half], int(own)
        wait(("rest", own, half), rest.at[o, :, ss])
        settle(LAST, ss, here, part[LAST, ss, y, :, here] + rest[o, 0, ss] + rest[o, 1, ss] + rest[o, 2, ss])

    homes = final.at[:, pl.ds(1, NZ - 1)]

    def flush():
        wait(("send", "spread"), amps.at[pl.ds(0, 6 * ROWS), pl.ds(0, PAIR)])
        wait(("send", "ring"), amps.at[pl.ds(0, 7 * SLOT_ROWS), :])
        wait(("send", "b"), ints.at[:, pl.ds(0, 7 * HALF), :])
        wait(("send", "p"), second)
        wait(("send", "q"), first)
        wait(("send", "rest"), rest)
        wait(("send", "home"), homes)

    ends = {}
    for part_of, own in (("O", True), ("F", False)):
        ends[f"{part_of}6P"] = functools.partial(last_p, own)
        ends[f"{part_of}6R"] = functools.partial(last_r, own, 1)
        ends[f"{part_of}6S"] = functools.partial(last_r, own, 0)
    for step, do in (("P", split_p), ("Q", split_q), ("R", split_r)):
        ends |= {f"O{j}{step}": functools.partial(do, j, True) for j in SPLIT[:-1]}
        ends |= {f"F{j}{step}": functools.partial(do, j, False) for j in SPLIT[:-1]}
    for event in ORDER:
        kind, which = event[0], event[1:]
        if event in ends:
            ends[event]()
        elif kind == "S":
            event_s(int(which))
        elif kind == "A":
            event_a(int(which[0]), int(which[1]))
        elif kind == "B":
            event_b(int(which[0]), int(which[1]))
        elif kind == "P":
            event_p(which)
        elif kind == "Q":
            event_q(which)
        else:
            event_r(which)

    wait("home", homes)
    for zz in range(NZ):
        for j in range(CHUNKS):
            for half in range(2):
                o_ref[:, pl.ds(zz * PAIR + half * BLOCK + j * LANES, LANES)] = landed[j, zz, :, pl.ds(half * LANES, LANES)]
    flush()
    assert len(names) == SEMS, len(names)


def body(amplitudes, integrals):
    return pl.pallas_call(
        kernel,
        out_shape=jax.ShapeDtypeStruct((ROWS, NZ * PAIR), BF16),
        in_specs=[pl.BlockSpec(memory_space=pl.ANY)] * 2,
        out_specs=pl.BlockSpec(memory_space=pltpu.VMEM),
        scratch_shapes=[
            pltpu.VMEM((NZ * SLOT_ROWS, DEEP), BF16),
            pltpu.VMEM((CHUNKS, DEEP, WIDE), BF16),
            pltpu.VMEM((CHUNKS, NZ, NY, ROWS, WIDE), F32),
            pltpu.VMEM((LAST, 2, NZ, ROWS, LANES), F32),
            pltpu.VMEM((LAST, 2, NZ, ROWS, WIDE), F32),
            pltpu.VMEM((CHUNKS, NZ, ROWS, WIDE), BF16),
            pltpu.VMEM((CHUNKS, NZ, ROWS, WIDE), BF16),
            pltpu.VMEM((2, NY - 1, NZ, ROWS, LANES), F32),
            pltpu.SemaphoreType.DMA((SEMS,)),
        ],
        compiler_params=pltpu.CompilerParams(collective_id=0, has_side_effects=True, vmem_limit_bytes=VMEM),
        cost_estimate=pl.CostEstimate(flops=2 * 512 * DEEP * PAIR, bytes_accessed=4 << 20, transcendentals=0),
    )(amplitudes, integrals)


def solution(mesh):
    return jax.shard_map(
        body,
        mesh=mesh,
        in_specs=(P(("col", "row"), None), P("col", "row")),
        out_specs=P(("col", "row"), None),
        check_vma=False,
    )
```

```python
import functools

import jax
import jax.numpy as jnp
from jax import lax
from jax.experimental import pallas as pl
from jax.experimental.pallas import tpu as pltpu
from jax.sharding import PartitionSpec as P

MESH = pl.DeviceIdType.MESH
BF16, F32 = jnp.bfloat16, jnp.float32

NX, NY, NZ = 4, 4, 8
ROWS = 16
BLOCK = 896
HALF = BLOCK // 2
LANES = 128
CHUNKS = BLOCK // LANES
WIDE = 2 * LANES
PAIR = 2 * BLOCK
DEEP = 4 * BLOCK
SLOTS = (0, 1, -1, 2, -2, 3, -3, 4)
SLOT_OF = {d: s for s, d in enumerate(SLOTS)}
SLOT_ROWS = NY * ROWS
VMEM = 427 << 17
SEMS = 83
SENDS = {
    None: ((0, 0), (0, 1), (1, 0)),
    0: ((1, 1), (2, 0)),
    1: ((2, 1), (3, 0)),
    2: ((3, 1), (4, 0)),
    3: ((4, 1), (5, 0)),
    4: ((5, 1),),
    5: ((6, 0), (6, 1)),
    6: (),
}

PASSES = {
    "a": (0, 1, 0, 3),
    "b": (1, 2, 0, 3),
    "c": (0, 2, 3, 5),
    "d": (2, 3, 0, 5),
    "e": (0, 3, 5, 7),
    "f": (3, 4, 0, 7),
    "g": (0, 4, 7, 8),
}
LAST = CHUNKS - 1
SPLIT = (4, 5, LAST)

ORDER = (
    "S1", "S3", "B00", "S2", "A10", "B01", "A11", "B10", "A13", "B02", "A12", "B03", "Pa", "B11", "A20", "B20",
    "A21", "B12", "A23", "B13", "Pb", "B21", "Qa", "A22", "B30", "Pc", "A30", "B22", "Qb", "Ra", "A31", "B23",
    "Pd", "B31", "Qc", "A33", "B40", "Rb", "A32", "Pe", "B32", "Qd", "B33", "Pf", "B41", "A40", "Qe", "B50",
    "O4P", "Rc", "Pg", "B42", "Rd", "B43", "F4P", "B51", "Qf", "O4Q", "B52", "Qg", "O5P", "B60", "B53", "F5P",
    "F4Q", "B61", "O6E", "Re", "O5Q", "O6P", "B62", "F6E", "O4R", "F5Q", "B63", "F6P", "Rf", "Rg", "F4R", "O5R",
    "O6R", "O6S", "F5R", "F6R", "F6S",
)


def kernel(a_ref, b_ref, o_ref, amps, ints, part, first, second, final, landed, rest, sems):
    row, col = lax.axis_index("row"), lax.axis_index("col")
    z, x = row // 2, (row % 2) * 2 + col // 8
    y, core = (col // 2) % NY, col % 2

    def at(dx=0, dy=0, dz=0, dk=0):
        xx, yy, zz, kk = (x + dx) % NX, (y + dy) % NY, (z + dz) % NZ, (core + dk) % 2
        return (zz * 2 + xx // 2, (xx % 2) * 8 + yy * 2 + kk)

    names = {}

    def sem(name):
        return names.setdefault(name, len(names))

    def put(send, recv, src, dst, to):
        pltpu.make_async_remote_copy(
            src_ref=src, dst_ref=dst, send_sem=sems.at[sem(("send", send))], recv_sem=sems.at[sem(recv)],
            device_id=to, device_id_type=MESH,
        ).start()

    def wait(name, like):
        pltpu.make_async_copy(like, like, sems.at[sem(name)]).wait()

    def place(j, dx, dk, r0, n):
        xx, kk = (x + dx) % NX, (core + dk) % 2
        rows = pl.multiple_of(((xx % 2) * 2 + kk) * BLOCK + r0, 16)
        return ints.at[j, pl.ds(rows, n), pl.ds(pl.multiple_of((xx // 2) * LANES, LANES), LANES)]

    for h in range(2):
        pltpu.make_async_copy(
            a_ref.at[:, pl.ds(pl.multiple_of(h * 4 * PAIR + y * PAIR, LANES), PAIR)],
            amps.at[pl.ds(pl.multiple_of(y * ROWS, ROWS), ROWS), pl.ds(h * PAIR, PAIR)],
            sems.at[sem("own a")],
        ).start()
    for j in range(CHUNKS):
        pltpu.make_async_copy(b_ref.at[:, pl.ds(j * LANES, LANES)], place(j, 0, 0, 0, BLOCK), sems.at[sem("own b")]).start()

    partners = [at(dx=1), at(dx=-1), at(dk=1)]
    partners += [at(dy=d) for d in range(1, NY)] + [at(dz=1), at(dz=-1)]
    barrier = pltpu.get_barrier_semaphore()
    for to in partners:
        pl.semaphore_signal(barrier, inc=1, device_id=to, device_id_type=MESH)
    pl.semaphore_wait(barrier, len(partners))

    def rows_of(d, dy):
        return pl.ds(pl.multiple_of(SLOT_OF[d] * SLOT_ROWS + (y + dy) % NY * ROWS, ROWS), ROWS)

    def hand_on(d, q):
        if d < 3 or q < 2:
            put("ring", ("ring", d + 1, q if d < 3 else 0), amps.at[rows_of(d, q), :], amps.at[rows_of(d + 1, q), :], at(dz=-1))
        if d < 3 or q >= 2:
            put("ring", ("ring", d + 1, q if d < 3 else 0), amps.at[rows_of(-d, q), :], amps.at[rows_of(4 if d == 3 else -(d + 1), q), :], at(dz=1))

    wait("own a", amps.at[pl.ds(0, ROWS), :])
    hand_on(0, 0)

    for d in (1, 3, 2):
        yy = (y + d) % NY
        for h in range(2):
            put(
                "spread",
                ("spread", NY - d),
                a_ref.at[:, pl.ds(pl.multiple_of(h * 4 * PAIR + yy * PAIR, LANES), PAIR)],
                amps.at[rows_of(0, 0), pl.ds(h * PAIR, PAIR)],
                at(dy=d),
            )

    def direct(j, step):
        for dx, r0 in ((1, step * HALF), (-1, (1 - step) * HALF)):
            put(
                "b", ("direct", j, step),
                b_ref.at[pl.ds(r0, HALF), pl.ds(j * LANES, LANES)], place(j, 0, 0, r0, HALF), at(dx=dx),
            )
        if step == 1:
            put("b", ("twin", j), b_ref.at[:, pl.ds(j * LANES, LANES)], place(j, 0, 0, 0, BLOCK), at(dk=1))

    for half in SENDS[None]:
        direct(*half)

    def event_s(q):
        wait(("spread", q), amps.at[pl.ds(0, ROWS), :])
        hand_on(0, q)

    def event_a(d, q):
        wait(("ring", d, q), amps.at[pl.ds(0, (4 if d == 4 else 2) * ROWS), :])
        if d < 4:
            hand_on(d, q)

    def event_b(j, step):
        two = ints.at[j, pl.ds(0, BLOCK), pl.ds(0, LANES)]
        if step == 0:
            wait(("direct", j, 0), two)
            for dx, r0 in ((1, 0), (-1, HALF)):
                put("b", ("onward", j), place(j, -dx, 0, r0, HALF), place(j, -dx, 0, r0, HALF), at(dx=dx))
            for half in SENDS[j]:
                direct(*half)
        elif step == 3:
            if j == 0:
                wait("own b", b_ref)
            if j in SPLIT:
                wait(("twin", j, "last"), two)
            else:
                wait(("twin", j), ints.at[j, :, pl.ds(0, LANES)])
        elif step == 1:
            wait(("direct", j, 1), two)
            for dx in (-1, 1):
                put("b", ("twin", j), place(j, dx, 0, 0, BLOCK), place(j, dx, 0, 0, BLOCK), at(dk=1))
        else:
            wait(("onward", j), two)
            name = ("twin", j, "last") if j in SPLIT else ("twin", j)
            put("b", name, place(j, 2, 0, 0, BLOCK), place(j, 2, 0, 0, BLOCK), at(dk=1))

    up, down, over = (y + 1) % NY, (y - 1) % NY, (y + 2) % NY
    LOW, HIGH = pl.ds(0, LANES), pl.ds(LANES, LANES)

    def event_p(p):
        j0, j1, s0, s1 = PASSES[p]
        js, ss = pl.ds(j0, j1 - j0), pl.ds(s0, s1 - s0)

        def one(j, carry):
            for m0, m1 in ((s0, s1),) if s1 - s0 < 6 else ((s0, NZ // 2), (NZ // 2, s1)):
                product = jnp.dot(amps[pl.ds(m0 * SLOT_ROWS, (m1 - m0) * SLOT_ROWS)], ints[j], preferred_element_type=F32)
                part[j, pl.ds(m0, m1 - m0)] = product.reshape(m1 - m0, NY, ROWS, WIDE)
            return carry

        if j1 - j0 == 1:
            one(j0, 0)
        else:
            lax.fori_loop(j0, j1, one, 0)
        put("p", ("far", p), part.at[js, ss, over, :, LOW], first.at[js, 0, ss], at(dy=1))
        put("p", ("far", p), part.at[js, ss, over, :, HIGH], first.at[js, 1, ss], at(dy=-1))
        put("p", ("near", p), part.at[js, ss, up, :, HIGH], second.at[js, 0, ss, :, HIGH], at(dy=1))
        put("p", ("near", p), part.at[js, ss, down, :, LOW], second.at[js, 1, ss, :, LOW], at(dy=-1))

    def event_q(p):
        j0, j1, s0, s1 = PASSES[p]
        js, ss = pl.ds(j0, j1 - j0), pl.ds(s0, s1 - s0)
        wait(("far", p), first.at[js, :, ss])
        first[js, 0, ss] += part[js, ss, up, :, LOW]
        put("q", ("near", p), first.at[js, 0, ss], second.at[js, 0, ss, :, LOW], at(dy=1))
        first[js, 1, ss] += part[js, ss, down, :, HIGH]
        put("q", ("near", p), first.at[js, 1, ss], second.at[js, 1, ss, :, HIGH], at(dy=-1))

    def event_r(p):
        j0, j1, s0, s1 = PASSES[p]
        js, ss = pl.ds(j0, j1 - j0), pl.ds(s0, s1 - s0)
        wait(("near", p), second.at[js, :, ss])
        total = part[js, ss, y] + second[js, 0, ss] + second[js, 1, ss]
        final[js, ss] = total.astype(BF16)
        for s in sorted(range(s0, s1), key=lambda s: -abs(SLOTS[s])):
            if s == 0:
                landed[js, z] = final[js, 0]
            else:
                put("home", "home", final.at[js, s], landed.at[js, z], at(dz=SLOTS[s]))

    def lane(own):
        return pl.ds(pl.multiple_of((x // 2 if own else 1 - x // 2) * LANES, LANES), LANES)

    def deep(near):
        return pl.ds(pl.multiple_of((1 - x % 2 if near else x % 2) * PAIR, LANES), PAIR)

    def share(j, ss, k, lanes, width):
        rows = pl.ds(ss.start * SLOT_ROWS, ss.size * SLOT_ROWS)
        product = jnp.dot(amps[rows, k], ints[j, k, lanes], preferred_element_type=F32)
        return product.reshape(ss.size, NY, ROWS, width)

    halves = (pl.ds(0, NZ // 2), pl.ds(NZ // 2, NZ // 2))

    def own_products(j):
        wait(("twin", j), ints.at[j, pl.ds(0, 3 * BLOCK), pl.ds(0, LANES)])
        for ss in halves:
            part[j, ss] = share(j, ss, deep(True), pl.ds(0, WIDE), WIDE)

    def split_p(j, own):
        u, d = halves if own else halves[::-1]
        here = lane(own)
        if own:
            own_products(j)
        for ss in halves:
            part[j, ss, :, :, here] += share(j, ss, deep(False), here, LANES)
        put("p", ("far", j, own), part.at[j, u, over, :, here], first.at[j, 0, u], at(dy=1))
        put("p", ("far", j, own), part.at[j, d, over, :, here], first.at[j, 1, d], at(dy=-1))
        put("p", ("near", j, own), part.at[j, d, up, :, here], second.at[j, 0, d, :, here], at(dy=1))
        put("p", ("near", j, own), part.at[j, u, down, :, here], second.at[j, 1, u, :, here], at(dy=-1))

    def split_q(j, own):
        u, d = halves if own else halves[::-1]
        here = lane(own)
        wait(("far", j, own), first.at[j, 0])
        first[j, 0, u] += part[j, u, up, :, here]
        put("q", ("near", j, own), first.at[j, 0, u], second.at[j, 0, u, :, here], at(dy=1))
        first[j, 1, d] += part[j, d, down, :, here]
        put("q", ("near", j, own), first.at[j, 1, d], second.at[j, 1, d, :, here], at(dy=-1))

    def settle(j, ss, here, total):
        final[j, ss, :, here] = total.astype(BF16)
        for s in range(ss.start + ss.size - 1, max(ss.start, 1) - 1, -1):
            put("home", "home", final.at[j, s, :, here], landed.at[j, z, :, here], at(dz=SLOTS[s]))
        if ss.start == 0:
            landed[j, z, :, here] = final[j, 0, :, here]

    def split_r(j, own):
        here = lane(own)
        wait(("near", j, own), second.at[j, 0])
        settle(j, pl.ds(0, NZ), here, part[j, :, y, :, here] + second[j, 0, :, :, here] + second[j, 1, :, :, here])

    def block(near, dk):
        xx = 1 - x % 2 if near else x % 2
        return pl.ds(pl.multiple_of((xx * 2 + (core + dk) % 2) * BLOCK, LANES), BLOCK)

    def last_e(own):
        here = lane(own)
        for ss in halves:
            if own:
                part[LAST, ss] = share(LAST, ss, block(True, 0), pl.ds(0, WIDE), WIDE)
            part[LAST, ss, :, :, here] += share(LAST, ss, block(False, 0), here, LANES)

    def last_p(own):
        here = lane(own)
        if own:
            wait(("twin", LAST), ints.at[LAST, pl.ds(0, 3 * BLOCK), pl.ds(0, LANES)])
        for half in (1, 0):
            ss = halves[half]
            if own:
                part[LAST, ss] += share(LAST, ss, block(True, 1), pl.ds(0, WIDE), WIDE)
            part[LAST, ss, :, :, here] += share(LAST, ss, block(False, 1), here, LANES)
            for d in (2, 1, 3):
                put("rest", ("rest", own, half), part.at[LAST, ss, (y + d) % NY, :, here], rest.at[int(own), d - 1, ss], at(dy=d))

    def last_r(own, half):
        here, ss, o = lane(own), halves[half], int(own)
        wait(("rest", own, half), rest.at[o, :, ss])
        settle(LAST, ss, here, part[LAST, ss, y, :, here] + rest[o, 0, ss] + rest[o, 1, ss] + rest[o, 2, ss])

    homes = final.at[:, pl.ds(1, NZ - 1)]

    def flush():
        wait(("send", "spread"), amps.at[pl.ds(0, 6 * ROWS), pl.ds(0, PAIR)])
        wait(("send", "ring"), amps.at[pl.ds(0, 7 * SLOT_ROWS), :])
        wait(("send", "b"), ints.at[:, pl.ds(0, 7 * HALF), :])
        wait(("send", "p"), second)
        wait(("send", "q"), first)
        wait(("send", "rest"), rest)
        wait(("send", "home"), homes)

    ends = {}
    for part_of, own in (("O", True), ("F", False)):
        ends[f"{part_of}6E"] = functools.partial(last_e, own)
        ends[f"{part_of}6P"] = functools.partial(last_p, own)
        ends[f"{part_of}6R"] = functools.partial(last_r, own, 1)
        ends[f"{part_of}6S"] = functools.partial(last_r, own, 0)
    for step, do in (("P", split_p), ("Q", split_q), ("R", split_r)):
        ends |= {f"O{j}{step}": functools.partial(do, j, True) for j in SPLIT[:-1]}
        ends |= {f"F{j}{step}": functools.partial(do, j, False) for j in SPLIT[:-1]}
    for event in ORDER:
        kind, which = event[0], event[1:]
        if event in ends:
            ends[event]()
        elif kind == "S":
            event_s(int(which))
        elif kind == "A":
            event_a(int(which[0]), int(which[1]))
        elif kind == "B":
            event_b(int(which[0]), int(which[1]))
        elif kind == "P":
            event_p(which)
        elif kind == "Q":
            event_q(which)
        else:
            event_r(which)

    wait("home", homes)
    for zz in range(NZ):
        for j in range(CHUNKS):
            for half in range(2):
                o_ref[:, pl.ds(zz * PAIR + half * BLOCK + j * LANES, LANES)] = landed[j, zz, :, pl.ds(half * LANES, LANES)]
    flush()
    assert len(names) == SEMS, len(names)


def body(amplitudes, integrals):
    return pl.pallas_call(
        kernel,
        out_shape=jax.ShapeDtypeStruct((ROWS, NZ * PAIR), BF16),
        in_specs=[pl.BlockSpec(memory_space=pl.ANY)] * 2,
        out_specs=pl.BlockSpec(memory_space=pltpu.VMEM),
        scratch_shapes=[
            pltpu.VMEM((NZ * SLOT_ROWS, DEEP), BF16),
            pltpu.VMEM((CHUNKS, DEEP, WIDE), BF16),
            pltpu.VMEM((CHUNKS, NZ, NY, ROWS, WIDE), F32),
            pltpu.VMEM((LAST, 2, NZ, ROWS, LANES), F32),
            pltpu.VMEM((LAST, 2, NZ, ROWS, WIDE), F32),
            pltpu.VMEM((CHUNKS, NZ, ROWS, WIDE), BF16),
            pltpu.VMEM((CHUNKS, NZ, ROWS, WIDE), BF16),
            pltpu.VMEM((2, NY - 1, NZ, ROWS, LANES), F32),
            pltpu.SemaphoreType.DMA((SEMS,)),
        ],
        compiler_params=pltpu.CompilerParams(collective_id=0, has_side_effects=True, vmem_limit_bytes=VMEM),
        cost_estimate=pl.CostEstimate(flops=2 * 512 * DEEP * PAIR, bytes_accessed=4 << 20, transcendentals=0),
    )(amplitudes, integrals)


def solution(mesh):
    return jax.shard_map(
        body,
        mesh=mesh,
        in_specs=(P(("col", "row"), None), P("col", "row")),
        out_specs=P(("col", "row"), None),
        check_vma=False,
    )
```

```python
import functools

import jax
import jax.numpy as jnp
from jax import lax
from jax.experimental import pallas as pl
from jax.experimental.pallas import tpu as pltpu
from jax.sharding import PartitionSpec as P

MESH = pl.DeviceIdType.MESH
BF16, F32 = jnp.bfloat16, jnp.float32

NX, NY, NZ = 4, 4, 8
ROWS = 16
BLOCK = 896
HALF = BLOCK // 2
LANES = 128
CHUNKS = BLOCK // LANES
WIDE = 2 * LANES
PAIR = 2 * BLOCK
DEEP = 4 * BLOCK
SLOTS = (0, 1, -1, 2, -2, 3, -3, 4)
SLOT_OF = {d: s for s, d in enumerate(SLOTS)}
SLOT_ROWS = NY * ROWS
VMEM = 427 << 17
SEMS = 83
SENDS = {
    None: ((0, 0), (0, 1), (1, 0)),
    0: ((1, 1), (2, 0)),
    1: ((2, 1), (3, 0)),
    2: ((3, 1), (4, 0)),
    3: ((4, 1), (5, 0)),
    4: ((5, 1),),
    5: ((6, 0), (6, 1)),
    6: (),
}

PASSES = {
    "a": (0, 1, 0, 3),
    "b": (1, 2, 0, 3),
    "c": (0, 2, 3, 5),
    "d": (2, 3, 0, 5),
    "e": (0, 3, 5, 7),
    "f": (3, 4, 0, 7),
    "g": (0, 4, 7, 8),
}
LAST = CHUNKS - 1
SPLIT = (4, 5, LAST)

ORDER = (
    "S1", "S3", "B00", "S2", "A10", "B01", "A11", "B10", "A13", "B02", "A12", "B03", "Pa", "B11", "A20", "B20",
    "A21", "B12", "A23", "B13", "Pb", "B21", "Qa", "A22", "B30", "Pc", "A30", "B22", "Qb", "Ra", "A31", "B23",
    "Pd", "B31", "Qc", "A33", "B40", "Rb", "A32", "Pe", "B32", "Qd", "B33", "Pf", "B41", "A40", "Qe", "B50",
    "O4P", "Rc", "B42", "Pg", "Rd", "B43", "F4P", "B51", "Qf", "O4Q", "B52", "O5P", "B60", "B53", "F5P", "Qg",
    "F4Q", "B61", "O6E", "Re", "O5Q", "O6P", "B62", "F6E", "O4R", "F5Q", "B63", "F6P", "Rf", "Rg", "F4R", "O5R",
    "O6R", "O6S", "F5R", "F6R", "F6S",
)


def kernel(a_ref, b_ref, o_ref, amps, ints, part, first, second, final, landed, rest, sems):
    row, col = lax.axis_index("row"), lax.axis_index("col")
    z, x = row // 2, (row % 2) * 2 + col // 8
    y, core = (col // 2) % NY, col % 2

    def at(dx=0, dy=0, dz=0, dk=0):
        xx, yy, zz, kk = (x + dx) % NX, (y + dy) % NY, (z + dz) % NZ, (core + dk) % 2
        return (zz * 2 + xx // 2, (xx % 2) * 8 + yy * 2 + kk)

    names = {}

    def sem(name):
        return names.setdefault(name, len(names))

    def put(send, recv, src, dst, to):
        pltpu.make_async_remote_copy(
            src_ref=src, dst_ref=dst, send_sem=sems.at[sem(("send", send))], recv_sem=sems.at[sem(recv)],
            device_id=to, device_id_type=MESH,
        ).start()

    def wait(name, like):
        pltpu.make_async_copy(like, like, sems.at[sem(name)]).wait()

    def place(j, dx, dk, r0, n):
        xx, kk = (x + dx) % NX, (core + dk) % 2
        rows = pl.multiple_of(((xx % 2) * 2 + kk) * BLOCK + r0, 16)
        return ints.at[j, pl.ds(rows, n), pl.ds(pl.multiple_of((xx // 2) * LANES, LANES), LANES)]

    for h in range(2):
        pltpu.make_async_copy(
            a_ref.at[:, pl.ds(pl.multiple_of(h * 4 * PAIR + y * PAIR, LANES), PAIR)],
            amps.at[pl.ds(pl.multiple_of(y * ROWS, ROWS), ROWS), pl.ds(h * PAIR, PAIR)],
            sems.at[sem("own a")],
        ).start()
    for j in range(CHUNKS):
        pltpu.make_async_copy(b_ref.at[:, pl.ds(j * LANES, LANES)], place(j, 0, 0, 0, BLOCK), sems.at[sem("own b")]).start()

    partners = [at(dx=1), at(dx=-1), at(dk=1)]
    partners += [at(dy=d) for d in range(1, NY)] + [at(dz=1), at(dz=-1)]
    barrier = pltpu.get_barrier_semaphore()
    for to in partners:
        pl.semaphore_signal(barrier, inc=1, device_id=to, device_id_type=MESH)
    pl.semaphore_wait(barrier, len(partners))

    def rows_of(d, dy):
        return pl.ds(pl.multiple_of(SLOT_OF[d] * SLOT_ROWS + (y + dy) % NY * ROWS, ROWS), ROWS)

    def hand_on(d, q):
        if d < 3 or q < 2:
            put("ring", ("ring", d + 1, q if d < 3 else 0), amps.at[rows_of(d, q), :], amps.at[rows_of(d + 1, q), :], at(dz=-1))
        if d < 3 or q >= 2:
            put("ring", ("ring", d + 1, q if d < 3 else 0), amps.at[rows_of(-d, q), :], amps.at[rows_of(4 if d == 3 else -(d + 1), q), :], at(dz=1))

    wait("own a", amps.at[pl.ds(0, ROWS), :])
    hand_on(0, 0)

    for d in (1, 3, 2):
        yy = (y + d) % NY
        for h in range(2):
            put(
                "spread",
                ("spread", NY - d),
                a_ref.at[:, pl.ds(pl.multiple_of(h * 4 * PAIR + yy * PAIR, LANES), PAIR)],
                amps.at[rows_of(0, 0), pl.ds(h * PAIR, PAIR)],
                at(dy=d),
            )

    def direct(j, step):
        for dx, r0 in ((1, step * HALF), (-1, (1 - step) * HALF)):
            put(
                "b", ("direct", j, step),
                b_ref.at[pl.ds(r0, HALF), pl.ds(j * LANES, LANES)], place(j, 0, 0, r0, HALF), at(dx=dx),
            )
        if step == 1:
            put("b", ("twin", j), b_ref.at[:, pl.ds(j * LANES, LANES)], place(j, 0, 0, 0, BLOCK), at(dk=1))

    for half in SENDS[None]:
        direct(*half)

    def event_s(q):
        wait(("spread", q), amps.at[pl.ds(0, ROWS), :])
        hand_on(0, q)

    def event_a(d, q):
        wait(("ring", d, q), amps.at[pl.ds(0, (4 if d == 4 else 2) * ROWS), :])
        if d < 4:
            hand_on(d, q)

    def event_b(j, step):
        two = ints.at[j, pl.ds(0, BLOCK), pl.ds(0, LANES)]
        if step == 0:
            wait(("direct", j, 0), two)
            for dx, r0 in ((1, 0), (-1, HALF)):
                put("b", ("onward", j), place(j, -dx, 0, r0, HALF), place(j, -dx, 0, r0, HALF), at(dx=dx))
            for half in SENDS[j]:
                direct(*half)
        elif step == 3:
            if j == 0:
                wait("own b", b_ref)
            if j in SPLIT:
                wait(("twin", j, "last"), two)
            else:
                wait(("twin", j), ints.at[j, :, pl.ds(0, LANES)])
        elif step == 1:
            wait(("direct", j, 1), two)
            for dx in (-1, 1):
                put("b", ("twin", j), place(j, dx, 0, 0, BLOCK), place(j, dx, 0, 0, BLOCK), at(dk=1))
        else:
            wait(("onward", j), two)
            name = ("twin", j, "last") if j in SPLIT else ("twin", j)
            put("b", name, place(j, 2, 0, 0, BLOCK), place(j, 2, 0, 0, BLOCK), at(dk=1))

    up, down, over = (y + 1) % NY, (y - 1) % NY, (y + 2) % NY
    LOW, HIGH = pl.ds(0, LANES), pl.ds(LANES, LANES)

    def event_p(p):
        j0, j1, s0, s1 = PASSES[p]
        js, ss = pl.ds(j0, j1 - j0), pl.ds(s0, s1 - s0)

        def one(j, carry):
            for m0, m1 in ((s0, s1),) if s1 - s0 < 6 else ((s0, NZ // 2), (NZ // 2, s1)):
                product = jnp.dot(amps[pl.ds(m0 * SLOT_ROWS, (m1 - m0) * SLOT_ROWS)], ints[j], preferred_element_type=F32)
                part[j, pl.ds(m0, m1 - m0)] = product.reshape(m1 - m0, NY, ROWS, WIDE)
            return carry

        if j1 - j0 == 1:
            one(j0, 0)
        else:
            lax.fori_loop(j0, j1, one, 0)
        put("p", ("far", p), part.at[js, ss, over, :, LOW], first.at[js, 0, ss], at(dy=1))
        put("p", ("far", p), part.at[js, ss, over, :, HIGH], first.at[js, 1, ss], at(dy=-1))
        put("p", ("near", p), part.at[js, ss, up, :, HIGH], second.at[js, 0, ss, :, HIGH], at(dy=1))
        put("p", ("near", p), part.at[js, ss, down, :, LOW], second.at[js, 1, ss, :, LOW], at(dy=-1))

    def event_q(p):
        j0, j1, s0, s1 = PASSES[p]
        js, ss = pl.ds(j0, j1 - j0), pl.ds(s0, s1 - s0)
        wait(("far", p), first.at[js, :, ss])
        first[js, 0, ss] += part[js, ss, up, :, LOW]
        put("q", ("near", p), first.at[js, 0, ss], second.at[js, 0, ss, :, LOW], at(dy=1))
        first[js, 1, ss] += part[js, ss, down, :, HIGH]
        put("q", ("near", p), first.at[js, 1, ss], second.at[js, 1, ss, :, HIGH], at(dy=-1))

    def event_r(p):
        j0, j1, s0, s1 = PASSES[p]
        js, ss = pl.ds(j0, j1 - j0), pl.ds(s0, s1 - s0)
        wait(("near", p), second.at[js, :, ss])
        total = part[js, ss, y] + second[js, 0, ss] + second[js, 1, ss]
        final[js, ss] = total.astype(BF16)
        for s in sorted(range(s0, s1), key=lambda s: -abs(SLOTS[s])):
            if s == 0:
                landed[js, z] = final[js, 0]
            else:
                put("home", "home", final.at[js, s], landed.at[js, z], at(dz=SLOTS[s]))

    def lane(own):
        return pl.ds(pl.multiple_of((x // 2 if own else 1 - x // 2) * LANES, LANES), LANES)

    def deep(near):
        return pl.ds(pl.multiple_of((1 - x % 2 if near else x % 2) * PAIR, LANES), PAIR)

    def share(j, ss, k, lanes, width):
        rows = pl.ds(ss.start * SLOT_ROWS, ss.size * SLOT_ROWS)
        product = jnp.dot(amps[rows, k], ints[j, k, lanes], preferred_element_type=F32)
        return product.reshape(ss.size, NY, ROWS, width)

    halves = (pl.ds(0, NZ // 2), pl.ds(NZ // 2, NZ // 2))

    def own_products(j):
        wait(("twin", j), ints.at[j, pl.ds(0, 3 * BLOCK), pl.ds(0, LANES)])
        for ss in halves:
            part[j, ss] = share(j, ss, deep(True), pl.ds(0, WIDE), WIDE)

    def split_p(j, own):
        u, d = halves if own else halves[::-1]
        here = lane(own)
        if own:
            own_products(j)
        for ss in halves:
            part[j, ss, :, :, here] += share(j, ss, deep(False), here, LANES)
        put("p", ("far", j, own), part.at[j, u, over, :, here], first.at[j, 0, u], at(dy=1))
        put("p", ("far", j, own), part.at[j, d, over, :, here], first.at[j, 1, d], at(dy=-1))
        put("p", ("near", j, own), part.at[j, d, up, :, here], second.at[j, 0, d, :, here], at(dy=1))
        put("p", ("near", j, own), part.at[j, u, down, :, here], second.at[j, 1, u, :, here], at(dy=-1))

    def split_q(j, own):
        u, d = halves if own else halves[::-1]
        here = lane(own)
        wait(("far", j, own), first.at[j, 0])
        first[j, 0, u] += part[j, u, up, :, here]
        put("q", ("near", j, own), first.at[j, 0, u], second.at[j, 0, u, :, here], at(dy=1))
        first[j, 1, d] += part[j, d, down, :, here]
        put("q", ("near", j, own), first.at[j, 1, d], second.at[j, 1, d, :, here], at(dy=-1))

    def settle(j, ss, here, total):
        final[j, ss, :, here] = total.astype(BF16)
        for s in range(ss.start + ss.size - 1, max(ss.start, 1) - 1, -1):
            put("home", "home", final.at[j, s, :, here], landed.at[j, z, :, here], at(dz=SLOTS[s]))
        if ss.start == 0:
            landed[j, z, :, here] = final[j, 0, :, here]

    def split_r(j, own):
        here = lane(own)
        wait(("near", j, own), second.at[j, 0])
        settle(j, pl.ds(0, NZ), here, part[j, :, y, :, here] + second[j, 0, :, :, here] + second[j, 1, :, :, here])

    def block(near, dk):
        xx = 1 - x % 2 if near else x % 2
        return pl.ds(pl.multiple_of((xx * 2 + (core + dk) % 2) * BLOCK, LANES), BLOCK)

    def last_e(own):
        here = lane(own)
        for ss in halves:
            if own:
                part[LAST, ss] = share(LAST, ss, block(True, 0), pl.ds(0, WIDE), WIDE)
            part[LAST, ss, :, :, here] += share(LAST, ss, block(False, 0), here, LANES)

    def last_p(own):
        here = lane(own)
        if own:
            wait(("twin", LAST), ints.at[LAST, pl.ds(0, 3 * BLOCK), pl.ds(0, LANES)])
        for half in (1, 0):
            ss = halves[half]
            if own:
                part[LAST, ss] += share(LAST, ss, block(True, 1), pl.ds(0, WIDE), WIDE)
            part[LAST, ss, :, :, here] += share(LAST, ss, block(False, 1), here, LANES)
            for d in (2, 1, 3):
                put("rest", ("rest", own, half), part.at[LAST, ss, (y + d) % NY, :, here], rest.at[int(own), d - 1, ss], at(dy=d))

    def last_r(own, half):
        here, ss, o = lane(own), halves[half], int(own)
        wait(("rest", own, half), rest.at[o, :, ss])
        settle(LAST, ss, here, part[LAST, ss, y, :, here] + rest[o, 0, ss] + rest[o, 1, ss] + rest[o, 2, ss])

    homes = final.at[:, pl.ds(1, NZ - 1)]

    def flush():
        wait(("send", "spread"), amps.at[pl.ds(0, 6 * ROWS), pl.ds(0, PAIR)])
        wait(("send", "ring"), amps.at[pl.ds(0, 7 * SLOT_ROWS), :])
        wait(("send", "b"), ints.at[:, pl.ds(0, 7 * HALF), :])
        wait(("send", "p"), second)
        wait(("send", "q"), first)
        wait(("send", "rest"), rest)
        wait(("send", "home"), homes)

    ends = {}
    for part_of, own in (("O", True), ("F", False)):
        ends[f"{part_of}6E"] = functools.partial(last_e, own)
        ends[f"{part_of}6P"] = functools.partial(last_p, own)
        ends[f"{part_of}6R"] = functools.partial(last_r, own, 1)
        ends[f"{part_of}6S"] = functools.partial(last_r, own, 0)
    for step, do in (("P", split_p), ("Q", split_q), ("R", split_r)):
        ends |= {f"O{j}{step}": functools.partial(do, j, True) for j in SPLIT[:-1]}
        ends |= {f"F{j}{step}": functools.partial(do, j, False) for j in SPLIT[:-1]}
    for event in ORDER:
        kind, which = event[0], event[1:]
        if event in ends:
            ends[event]()
        elif kind == "S":
            event_s(int(which))
        elif kind == "A":
            event_a(int(which[0]), int(which[1]))
        elif kind == "B":
            event_b(int(which[0]), int(which[1]))
        elif kind == "P":
            event_p(which)
        elif kind == "Q":
            event_q(which)
        else:
            event_r(which)

    wait("home", homes)
    for zz in range(NZ):
        for j in range(CHUNKS):
            for half in range(2):
                o_ref[:, pl.ds(zz * PAIR + half * BLOCK + j * LANES, LANES)] = landed[j, zz, :, pl.ds(half * LANES, LANES)]
    flush()
    assert len(names) == SEMS, len(names)


def body(amplitudes, integrals):
    return pl.pallas_call(
        kernel,
        out_shape=jax.ShapeDtypeStruct((ROWS, NZ * PAIR), BF16),
        in_specs=[pl.BlockSpec(memory_space=pl.ANY)] * 2,
        out_specs=pl.BlockSpec(memory_space=pltpu.VMEM),
        scratch_shapes=[
            pltpu.VMEM((NZ * SLOT_ROWS, DEEP), BF16),
            pltpu.VMEM((CHUNKS, DEEP, WIDE), BF16),
            pltpu.VMEM((CHUNKS, NZ, NY, ROWS, WIDE), F32),
            pltpu.VMEM((LAST, 2, NZ, ROWS, LANES), F32),
            pltpu.VMEM((LAST, 2, NZ, ROWS, WIDE), F32),
            pltpu.VMEM((CHUNKS, NZ, ROWS, WIDE), BF16),
            pltpu.VMEM((CHUNKS, NZ, ROWS, WIDE), BF16),
            pltpu.VMEM((2, NY - 1, NZ, ROWS, LANES), F32),
            pltpu.SemaphoreType.DMA((SEMS,)),
        ],
        compiler_params=pltpu.CompilerParams(collective_id=0, has_side_effects=True, vmem_limit_bytes=VMEM),
        cost_estimate=pl.CostEstimate(flops=2 * 512 * DEEP * PAIR, bytes_accessed=4 << 20, transcendentals=0),
    )(amplitudes, integrals)


def solution(mesh):
    return jax.shard_map(
        body,
        mesh=mesh,
        in_specs=(P(("col", "row"), None), P("col", "row")),
        out_specs=P(("col", "row"), None),
        check_vma=False,
    )
```
